512 devices in a mesh: fsdp: 32 (over z_hi, x, core), sp: 16 (over z_lo, y).
Axes of the slice: x: 4, y: 8, z: 8 (z_hi: 4, z_lo: 2; z = z_hi * 2 + z_lo), core: 2. Of those that a mesh axis runs over, the one named last changes fastest.
Arguments:
- query: bfloat16 [65536, 2048], P(('fsdp', 'sp')), may hold values from -6 to 6
- projected_key_rows: bfloat16 [65536, 2048], P(('fsdp', 'sp')), may hold values from -6 to 6
- value: bfloat16 [65536, 2048], P(('fsdp', 'sp')), may hold values from -6 to 6
- blocks: int32 [32, 16, 6], P('fsdp'), may hold values from 0 to 15, as said below
- frozen_output_weight: bfloat16 [2048, 2048], P('fsdp'), may hold values from -0.125 to 0.125
- adapter_down_weight: bfloat16 [2048, 64], P('fsdp'), may hold values from -0.125 to 0.125
- adapter_up_weight_transposed: bfloat16 [2048, 64], P('fsdp'), may hold values from -0.75 to 0.75
- cotangent: bfloat16 [65536, 2048], P(('fsdp', 'sp')), may hold values from -24 to 24
Outputs:
- mixed: bfloat16 [65536, 2048], P(('fsdp', 'sp'))
- grad_query: bfloat16 [65536, 2048], P(('fsdp', 'sp'))
- grad_key: bfloat16 [65536, 2048], P(('fsdp', 'sp'))
- grad_value: bfloat16 [65536, 2048], P(('fsdp', 'sp'))
- grad_down: float32 [2048, 64], P('fsdp')
- grad_up: float32 [2048, 64], P('fsdp')
The draws below stay inside these ranges and needn't reach their ends.
Inputs may be any that keep to these rules, and one draw needn't show every extreme that they name: Entry 1 of each list is the query block itself, entries 0 and 2 its neighbours (wrapping at the ends), entry 3 one block common to all query blocks of the sequence, the rest any blocks.
All inputs are finite; a program needn't handle non-finite values.
Results may differ from the reference program's by a relative error of at most 0.0081.
Values may be sent and summed in bfloat16 or wider, within the bound.
A program may use at most 128 MiB of HBM per device.

```python
import math
import jax
import jax.numpy as jnp
from jax import lax

MODEL_WIDTH = 2048
HEADS = 16
BLOCK = 128
KEY_BLOCKS = 6
ADAPTER_RANK = 64
NBLOCKS = 16
SEQS = 32
TOKENS = 65536


def drawn_pair(key):
    first = jnp.clip(jax.random.normal(jax.random.fold_in(key, 101), (TOKENS, MODEL_WIDTH), jnp.float32), -6.0, 6.0)
    second = jnp.clip(jax.random.normal(jax.random.fold_in(key, 202), (TOKENS, MODEL_WIDTH), jnp.float32), -6.0, 6.0)
    return (first, second)


def draw_query(key, part):
    return drawn_pair(key)[0].astype(jnp.bfloat16)


def draw_projected_key_rows(key, part):
    return drawn_pair(key)[1].astype(jnp.bfloat16)


def draw_blocks(key, part):
    count = NBLOCKS
    index_row = jnp.arange(count, dtype=jnp.int32)
    window = jnp.stack([(index_row - 1) % count, index_row, (index_row + 1) % count], axis=-1)
    window = jnp.broadcast_to(window[None, :, :], (SEQS, count, 3))
    common = jax.random.randint(jax.random.fold_in(key, 404), (SEQS, 1, 1), 0, count, dtype=jnp.int32)
    common = jnp.broadcast_to(common, (SEQS, count, 1))
    random_part = jax.random.randint(jax.random.fold_in(key, 505), (SEQS, count, KEY_BLOCKS - 4), 0, count, dtype=jnp.int32)
    return jnp.concatenate([window, common, random_part], axis=-1).astype(jnp.int32)


def with_spikes(values, rng, source, target, blocks, factor):
    def block_of(dim):
        return (jnp.arange(values.shape[dim]) // (values.shape[dim] // blocks)).reshape((-1,) + (1,) * (values.ndim - 1 - dim))

    first = jax.random.permutation(rng, blocks)[block_of(target)]
    other_side = (block_of(target) + blocks // 2) % blocks
    return jnp.where((block_of(source) == first) | (block_of(source) == other_side), factor * values, values)


def block_levels(key, extent, split, least, top_value):
    gain = 1.0
    for position, shards_of in split:
        steps = jax.random.uniform(jax.random.fold_in(jax.random.fold_in(key, 6), position), (shards_of,), jnp.float32, least / len(split), top_value / len(split))
        gain = gain * jnp.repeat(jnp.exp(steps), extent[position] // shards_of).reshape((-1,) + (1,) * (len(extent) - 1 - position))
    return gain


def noise(rng, shape, scale, most, pieces=(), kind=jnp.bfloat16):
    entries = jax.random.normal(rng, shape, jnp.float32) * scale
    if len(pieces) > 0:
        entries = block_levels(rng, shape, pieces, -0.22, 0.18) * entries
    return jnp.clip(entries, min=-most, max=most).astype(kind)


def bell_draw_with(rng, dims, spread, most, pieces, heavy, held_as=jnp.bfloat16):
    drawn = spread * jax.random.normal(rng, dims, jnp.float32)
    if pieces:
        drawn = drawn * block_levels(rng, dims, pieces, -0.22, 0.18)
    return jnp.clip(with_spikes(drawn, jax.random.fold_in(rng, 3), *heavy), -most, most).astype(held_as)


def setup_inputs(seed: int = 0) -> dict:
    key_list = jax.random.split(jax.random.key(seed), 9)
    return {
        "query": draw_query(jax.random.fold_in(key_list[8], 71), 0),
        "projected_key_rows": draw_projected_key_rows(jax.random.fold_in(key_list[8], 71), 0),
        "value": noise(key_list[2], (TOKENS, MODEL_WIDTH), 1.0, 6.0, ((0, 512),)),
        "blocks": draw_blocks(jax.random.fold_in(key_list[8], 71), 0),
        "frozen_output_weight": noise(key_list[4], (MODEL_WIDTH, MODEL_WIDTH), MODEL_WIDTH ** -0.5, 0.125, ((0, 32),)),
        "adapter_down_weight": noise(key_list[5], (MODEL_WIDTH, ADAPTER_RANK), MODEL_WIDTH ** -0.5, 0.125, ((0, 32),)),
        "adapter_up_weight_transposed": noise(key_list[6], (MODEL_WIDTH, ADAPTER_RANK), ADAPTER_RANK ** -0.5, 0.75, ((0, 32),)),
        "cotangent": bell_draw_with(key_list[7], (TOKENS, MODEL_WIDTH), 1.0, 24.0, ((0, 512),), (0, 1, 512, 6.0)),
    }


def attend_sequence(query, projected_key_rows, value, lists):
    count = lists.shape[0]
    head_dim = MODEL_WIDTH // HEADS
    scaling = 1.0 / math.sqrt(head_dim)
    query_blocks = query.astype(jnp.float32).reshape(count, BLOCK, HEADS, head_dim)
    key_blocks = projected_key_rows.astype(jnp.float32).reshape(count, BLOCK, HEADS, head_dim)
    value_blocks = value.astype(jnp.float32).reshape(count, BLOCK, HEADS, head_dim)
    listed = lists.reshape(-1).astype(jnp.int32)
    keys_gathered = jnp.take(key_blocks, listed, axis=0).reshape(count, KEY_BLOCKS * BLOCK, HEADS, head_dim)
    values_gathered = jnp.take(value_blocks, listed, axis=0).reshape(count, KEY_BLOCKS * BLOCK, HEADS, head_dim)
    scores = jnp.einsum('gqhd,gkhd->ghqk', query_blocks, keys_gathered) * scaling
    highest = lax.optimization_barrier(jnp.max(scores, axis=-1, keepdims=True))
    raised = jnp.exp(scores - highest)
    probs = raised / lax.optimization_barrier(jnp.sum(raised, axis=-1, keepdims=True))
    weights = probs.astype(jnp.bfloat16)
    attended_context = jnp.einsum('ghqk,gkhd->gqhd', weights.astype(jnp.float32), values_gathered).astype(jnp.bfloat16)
    return (attended_context.reshape(count * BLOCK, MODEL_WIDTH), probs, weights, keys_gathered, values_gathered, query_blocks)

def attend_backward(query, projected_key_rows, value, lists, attended_context_gradient):
    count = lists.shape[0]
    head_dim = MODEL_WIDTH // HEADS
    scaling = 1.0 / math.sqrt(head_dim)
    unused, probs, weights, keys_gathered, values_gathered, query_blocks = attend_sequence(query, projected_key_rows, value, lists)
    grad_blocks = attended_context_gradient.astype(jnp.float32).reshape(count, BLOCK, HEADS, head_dim)
    dweights = jnp.einsum('gqhd,gkhd->ghqk', grad_blocks, values_gathered)
    correction = lax.optimization_barrier(jnp.sum(probs * dweights, axis=-1, keepdims=True))
    dscores = (probs * (dweights - correction) * scaling).astype(jnp.bfloat16)
    grad_query = jnp.einsum('ghqk,gkhd->gqhd', dscores.astype(jnp.float32), keys_gathered).astype(jnp.bfloat16)
    key_terms = jnp.einsum('ghqk,gqhd->gkhd', dscores.astype(jnp.float32), query_blocks)
    value_terms = jnp.einsum('ghqk,gqhd->gkhd', weights.astype(jnp.float32), grad_blocks)
    listed = lists.reshape(-1).astype(jnp.int32)
    one_hot = (listed[:, None] == jnp.arange(count, dtype=jnp.int32)[None, :]).astype(jnp.float32)
    grad_key = jnp.einsum('in,ij->nj', one_hot, key_terms.reshape(count * KEY_BLOCKS, BLOCK * MODEL_WIDTH), precision=lax.Precision.HIGHEST)
    grad_value = jnp.einsum('in,ij->nj', one_hot, value_terms.reshape(count * KEY_BLOCKS, BLOCK * MODEL_WIDTH), precision=lax.Precision.HIGHEST)
    return (grad_query.reshape(count * BLOCK, MODEL_WIDTH), grad_key.reshape(count * BLOCK, MODEL_WIDTH).astype(jnp.bfloat16), grad_value.reshape(count * BLOCK, MODEL_WIDTH).astype(jnp.bfloat16))

def reference(query, projected_key_rows, value, blocks, frozen_output_weight, adapter_down_weight, adapter_up_weight_transposed, cotangent):
    sequences = blocks.shape[0]
    length = query.shape[0] // sequences

    def shaped(array):
        return array.reshape(sequences, length, MODEL_WIDTH)
    attended_context = lax.map(lambda items: attend_sequence(items[0], items[1], items[2], items[3])[0], (shaped(query), shaped(projected_key_rows), shaped(value), blocks)).reshape(-1, MODEL_WIDTH)
    reduced_rank_output = jnp.dot(attended_context, adapter_down_weight, preferred_element_type=jnp.float32).astype(jnp.bfloat16)
    mixed = (jnp.dot(attended_context, frozen_output_weight, preferred_element_type=jnp.float32) + jnp.dot(reduced_rank_output, adapter_up_weight_transposed.T, preferred_element_type=jnp.float32)).astype(jnp.bfloat16)
    reduced_gradient = jnp.dot(cotangent, adapter_up_weight_transposed, preferred_element_type=jnp.float32).astype(jnp.bfloat16)
    attended_context_gradient = (jnp.dot(cotangent, frozen_output_weight.T, preferred_element_type=jnp.float32) + jnp.dot(reduced_gradient, adapter_down_weight.T, preferred_element_type=jnp.float32)).astype(jnp.bfloat16)
    normal_factor = 1.0 / math.sqrt(TOKENS)
    grad_down = jnp.dot(attended_context.T, reduced_gradient, preferred_element_type=jnp.float32) * normal_factor
    grad_up = jnp.dot(cotangent.T, reduced_rank_output, preferred_element_type=jnp.float32) * normal_factor
    grad_query, grad_key, grad_value = lax.map(lambda items: attend_backward(items[0], items[1], items[2], items[3], items[4]), (shaped(query), shaped(projected_key_rows), shaped(value), blocks, shaped(attended_context_gradient)))
    return (mixed, grad_query.reshape(-1, MODEL_WIDTH), grad_key.reshape(-1, MODEL_WIDTH), grad_value.reshape(-1, MODEL_WIDTH), grad_down, grad_up)
```

```python
import math

import jax
import jax.numpy as jnp
from jax import lax
from jax.experimental import pallas as pl
from jax.experimental.pallas import tpu as pltpu
from jax.sharding import PartitionSpec as P

MODEL_WIDTH = 2048
HEADS = 16
BLOCK = 128
KEY_BLOCKS = 6
ADAPTER_RANK = 64
TOKENS = 65536

NZ, NX = 4, 4
NL, NY = 2, 8
NB = NL * NY
SHARD = 64
RANDOM = 2 * NB

MESH = pl.DeviceIdType.MESH
F32 = jnp.float32
BF16 = jnp.bfloat16


def dot(a, b, ca, cb):
    return lax.dot_general(a, b, (((ca,), (cb,)), ((), ())), preferred_element_type=F32)


def drain(ref, sem):
    pltpu.make_async_copy(ref, ref, sem).wait()


def kernel(
    q_ref,
    k_ref,
    v_ref,
    blk,
    w_ref,
    a_ref,
    b_ref,
    cot,
    mixed_ref,
    dq_ref,
    dk_ref,
    dv_ref,
    gd_ref,
    gu_ref,
    qh,
    kh,
    vh,
    gh,
    ctx_heads,
    dctx_send,
    ctx,
    dqb,
    dkb,
    dvb,
    wfull,
    ab,
    probs,
    wts,
    dsc,
    pre_k,
    pre_v,
    d0,
    part,
    rc,
    s1,
    rx,
    s2,
    rz,
    s3,
    rl,
    s4,
    ry,
    s5,
    gfin,
    rank,
    perm,
    same,
    last,
    has,
    qkv_s,
    qkv_r,
    blk_s,
    blk_r,
    abz_s,
    abz_r,
    wz_s,
    wz_r,
    wx_s,
    wx_r,
    wc_s,
    wc_r,
    own_sem,
    red_s,
    red_r,
):
    f = lax.axis_index("fsdp")
    j = lax.axis_index("sp")
    z, x, c = f // (2 * NX), (f // 2) % NX, f % 2
    zl, y = j // NY, j % NY
    oc = 1 - c
    scaling = 1.0 / math.sqrt(BLOCK)
    log2e = 1.4426950408889634

    def fid(zz, xx, cc):
        return zz * (2 * NX) + xx * 2 + cc

    def sp_peer(d):
        return (j + d) % NB

    sibling = (fid(z, x, oc), j)

    def xpeer(d):
        return (fid(z, (x + d) % NX, c), j)

    def zpeer(d):
        return (fid((z + d) % NZ, x, c), j)

    def remote(src, dst, ssem, rsem, dev):
        pltpu.make_async_remote_copy(
            src_ref=src, dst_ref=dst, send_sem=ssem, recv_sem=rsem, device_id=dev, device_id_type=MESH
        ).start()

    def cols(h):
        return pl.ds(pl.multiple_of(h * BLOCK, BLOCK), BLOCK)

    barrier = pltpu.get_barrier_semaphore()

    def greet(d, carry):
        pl.semaphore_signal(barrier, inc=1, device_id=(f, sp_peer(d)), device_id_type=MESH)
        return carry

    lax.fori_loop(1, NB, greet, 0)
    for d in (1, 2, 3):
        pl.semaphore_signal(barrier, inc=1, device_id=xpeer(d), device_id_type=MESH)
        pl.semaphore_signal(barrier, inc=1, device_id=zpeer(d), device_id_type=MESH)
    pl.semaphore_signal(barrier, inc=1, device_id=sibling, device_id_type=MESH)
    pl.semaphore_wait(barrier, NB - 1 + 7)

    ab[z, x, c] = jnp.concatenate([a_ref[...], b_ref[...]], axis=1)
    for d in (1, 3, 2):
        remote(ab.at[z, x, c], ab.at[z, x, c], abz_s.at[0], abz_r.at[0], zpeer(d))

    for n, (src, dst) in enumerate(((k_ref, kh), (q_ref, qh), (v_ref, vh))):

        def send_heads(d, carry, src=src, dst=dst, n=n):
            h = sp_peer(d)
            remote(src.at[:, cols(h)], dst.at[j], qkv_s.at[n], qkv_r.at[n], (f, h))
            return carry

        lax.fori_loop(1, NB, send_heads, 0)
        pltpu.make_async_copy(src.at[:, cols(j)], dst.at[j], qkv_r.at[n]).start()
        if n == 0:
            for d in (1, 3, 2):
                remote(w_ref, wfull.at[z, x, c], wz_s, wz_r.at[z], zpeer(d))
            pltpu.make_async_copy(w_ref, wfull.at[z, x, c], own_sem).start()
            remote(w_ref, wfull.at[z, x, c], wc_s, wc_r.at[z, x], sibling)
            drain(ab.at[0, pl.ds(0, 3), 0], abz_r.at[0])
            for d in (1, 3, 2):
                remote(ab.at[:, x, c], ab.at[:, x, c], abz_s.at[1], abz_r.at[1], xpeer(d))
            for d in (1, 3, 2):
                remote(w_ref, wfull.at[z, x, c], wx_s, wx_r.at[z, x], xpeer(d))

    def entry(r):
        return blk[0, r // 2, 4 + r % 2]

    def rank_of(r, carry):
        mine = entry(r) * RANDOM + r
        total = jnp.int32(0)
        for s in range(RANDOM):
            total = total + jnp.where(entry(s) * RANDOM + s < mine, 1, 0)
        rank[r] = total
        return carry

    lax.fori_loop(0, RANDOM, rank_of, 0)

    def perm_of(p, carry):
        total = jnp.int32(0)
        for s in range(RANDOM):
            total = total + jnp.where(rank[s] == p, s, 0)
        perm[p] = total
        named = blk[0, total // 2, 4 + total % 2]
        same[p] = jnp.where(named == carry, 1.0, 0.0).astype(F32)
        return named

    lax.fori_loop(0, RANDOM, perm_of, jnp.int32(-1))

    def last_of(n, carry):
        upto = jnp.int32(0)
        equal = jnp.int32(0)
        for s in range(RANDOM):
            upto = upto + jnp.where(entry(s) <= n, 1, 0)
            equal = equal + jnp.where(entry(s) == n, 1, 0)
        last[n] = jnp.maximum(upto - 1, 0)
        has[n] = jnp.where(equal > 0, 1.0, 0.0).astype(F32)
        return carry

    lax.fori_loop(0, NB, last_of, 0)

    drain(ab.at[pl.ds(0, 3), :, 0], abz_r.at[1])
    remote(ab.at[:, :, c], ab.at[:, :, c], abz_s.at[2], abz_r.at[2], sibling)

    def forward_z(d):
        u = (z + d) % NZ
        piece = wfull.at[u, x, c]
        drain(piece, wz_r.at[u])
        for e in (1, 3, 2):
            remote(piece, piece, wx_s, wx_r.at[u, x], xpeer(e))
        remote(piece, piece, wc_s, wc_r.at[u, x], sibling)

    def forward_x(d):
        u = (z + d) % NZ
        for e in (1, 3, 2):
            xx = (x + e) % NX
            piece = wfull.at[u, xx, c]
            drain(piece, wx_r.at[u, xx])
            remote(piece, piece, wc_s, wc_r.at[u, xx], sibling)

    def context_gradient(d):
        u = (z + d) % NZ

        def one_head(e, carry):
            xx = (x + e) % NX
            h = u * NX + xx
            drain(wfull.at[u, xx, oc], wc_r.at[u, xx])
            rows = wfull[u, xx].reshape(BLOCK, MODEL_WIDTH)
            adapter = ab[u, xx].reshape(BLOCK, 2 * ADAPTER_RANK)
            g = dot(cot[...], rows, 1, 1) + dot(d0[...], adapter, 1, 1)
            dctx_send[h] = g.astype(BF16)

            @pl.when(h != j)
            def _():
                remote(dctx_send.at[h], gh.at[j], blk_s.at[1], blk_r.at[1], (f, h))

            @pl.when(h == j)
            def _():
                pltpu.make_async_copy(dctx_send.at[h], gh.at[j], blk_r.at[1]).start()

            return carry

        lax.fori_loop(0, NX, one_head, 0)

    forward_z(1)
    forward_z(3)
    forward_x(0)

    drain(w_ref, own_sem)
    drain(ab.at[:, :, 0], abz_r.at[2])
    lane = lax.broadcasted_iota(jnp.int32, (BLOCK, 2 * ADAPTER_RANK), 1)
    both = dot(cot[...], ab[...].reshape(MODEL_WIDTH, 2 * ADAPTER_RANK), 1, 0)
    d0[...] = jnp.where(lane < ADAPTER_RANK, pltpu.roll(both, ADAPTER_RANK, 1), 0.0).astype(BF16)

    context_gradient(0)
    forward_z(2)
    forward_x(1)
    forward_x(3)
    context_gradient(1)

    drain(kh, qkv_r.at[0])
    drain(qh, qkv_r.at[1])
    drain(vh, qkv_r.at[2])

    def gathered(ref, i):
        return jnp.concatenate([ref[blk[0, i, s]] for s in range(KEY_BLOCKS)], axis=0)

    def send_block(src, dst_ref, n, i):
        @pl.when(i != j)
        def _():
            remote(src.at[i], dst_ref.at[:, cols(j)], blk_s.at[n], blk_r.at[n], (f, i))

        @pl.when(i == j)
        def _():
            pltpu.make_async_copy(src.at[i], dst_ref.at[:, cols(j)], blk_r.at[n]).start()

    def forward_block(t, carry):
        i = sp_peer(t)
        scores = dot(gathered(kh, i), qh[i], 1, 1)
        highest = jnp.max(scores, axis=0, keepdims=True)
        raised = jnp.exp2((scores - highest) * (scaling * log2e))
        p = raised * (1.0 / jnp.sum(raised, axis=0, keepdims=True))
        probs[i] = p
        w = p.astype(BF16)
        wts[i] = w.reshape(KEY_BLOCKS, BLOCK, BLOCK)
        ctx_heads[i] = dot(w, gathered(vh, i), 0, 0).astype(BF16)
        send_block(ctx_heads, ctx, 0, i)
        return carry

    lax.fori_loop(1, NB + 1, forward_block, 0)

    context_gradient(3)
    forward_x(2)
    context_gradient(2)
    drain(gh, blk_r.at[1])

    def backward_block(t, carry):
        i = sp_peer(t)
        p = probs[i]
        dw = dot(gathered(vh, i), gh[i], 1, 1)
        correction = jnp.sum(p * dw, axis=0, keepdims=True)
        ds = (p * (dw - correction) * scaling).astype(BF16)
        dsc[i] = ds.reshape(KEY_BLOCKS, BLOCK, BLOCK)
        dqb[i] = dot(ds, gathered(kh, i), 0, 0).astype(BF16)
        send_block(dqb, dq_ref, 2, i)
        return carry

    lax.fori_loop(1, NB + 1, backward_block, 0)

    def random_terms(p, carry):
        r = perm[p]
        i = r // 2
        slot = 4 + r % 2
        keep = same[p]
        acc_k = carry[0] * keep + dot(dsc[i, slot], qh[i], 1, 0)
        acc_v = carry[1] * keep + dot(wts[i, slot], gh[i], 1, 0)
        pre_k[p] = acc_k
        pre_v[p] = acc_v
        return acc_k, acc_v

    zero = jnp.zeros((BLOCK, BLOCK), F32)
    lax.fori_loop(0, RANDOM, random_terms, (zero, zero))

    def common_terms(i, carry):
        return (
            carry[0] + dot(dsc[i, 3], qh[i], 1, 0),
            carry[1] + dot(wts[i, 3], gh[i], 1, 0),
        )

    common_k, common_v = lax.fori_loop(0, NB, common_terms, (zero, zero))
    pre_k[RANDOM] = common_k
    pre_v[RANDOM] = common_v
    common = blk[0, 0, 3]

    def key_block(t, carry):
        n = sp_peer(t)
        before, after = (n + NB - 1) % NB, (n + 1) % NB
        slot_before = jnp.where(blk[0, before, 2] == n, 2, 0)
        slot_after = jnp.where(blk[0, after, 0] == n, 0, 2)
        is_common = jnp.where(common == n, 1.0, 0.0).astype(F32)

        def total(terms, rows, pre):
            window = (
                dot(terms[n, 1], rows[n], 1, 0)
                + dot(terms[before, slot_before], rows[before], 1, 0)
                + dot(terms[after, slot_after], rows[after], 1, 0)
            )
            return (window + pre[last[n]] * has[n] + pre[RANDOM] * is_common).astype(BF16)

        dkb[n] = total(dsc, qh, pre_k)
        send_block(dkb, dk_ref, 3, n)
        dvb[n] = total(wts, gh, pre_v)
        send_block(dvb, dv_ref, 4, n)
        return carry

    lax.fori_loop(1, NB + 1, key_block, 0)

    drain(ctx, blk_r.at[0])
    both = dot(ctx[...], ab[...].reshape(MODEL_WIDTH, 2 * ADAPTER_RANK), 1, 0)
    low = jnp.where(lane >= ADAPTER_RANK, pltpu.roll(both, ADAPTER_RANK, 1), 0.0).astype(BF16)
    normal = 1.0 / math.sqrt(TOKENS)

    def partial(h, carry):
        s = dot(ctx[:, cols(h)], d0[...], 0, 0) + dot(cot[:, cols(h)], low, 0, 0)
        part[h // NX, h % NX] = (s * normal).reshape(2, SHARD, BLOCK)
        return carry

    lax.fori_loop(0, HEADS, partial, 0)
    remote(part.at[:, :, oc], rc, red_s.at[0], red_r.at[0], sibling)

    wide = 256

    def output_columns(n, carry):
        rows = wfull[:, :, :, :, pl.ds(pl.multiple_of(n * wide, wide), wide)]
        adapter = ab[n // 2, pl.ds(2 * (n % 2), 2)].reshape(wide, 2 * ADAPTER_RANK)
        m = dot(ctx[...], rows.reshape(MODEL_WIDTH, wide), 1, 0) + dot(low, adapter, 1, 1)
        mixed_ref[:, pl.ds(pl.multiple_of(n * wide, wide), wide)] = m.astype(BF16)
        return carry

    lax.fori_loop(0, MODEL_WIDTH // wide, output_columns, 0)

    drain(rc, red_r.at[0])

    def add_core(u, carry):
        s1[u] = part[u, :, c] + rc[u]
        return carry

    lax.fori_loop(0, NZ, add_core, 0)
    for e in (1, 3, 2):
        remote(s1.at[:, (x + e) % NX], rx.at[x], red_s.at[1], red_r.at[1], xpeer(e))
    drain(rx.at[pl.ds(0, 3)], red_r.at[1])
    s2[...] = s1[:, x] + rx[(x + 1) % NX] + rx[(x + 2) % NX] + rx[(x + 3) % NX]
    for e in (1, 3, 2):
        remote(s2.at[(z + e) % NZ], rz.at[z], red_s.at[2], red_r.at[2], zpeer(e))
    drain(rz.at[pl.ds(0, 3)], red_r.at[2])
    s3[...] = s2[z] + rz[(z + 1) % NZ] + rz[(z + 2) % NZ] + rz[(z + 3) % NZ]
    remote(s3, rl, red_s.at[3], red_r.at[3], (f, (1 - zl) * NY + y))
    drain(rl, red_r.at[3])
    s4[...] = (s3[...] + rl[...]).reshape(NY, 8, BLOCK)
    for e in range(1, NY):
        yy = (y + e) % NY
        remote(s4.at[yy], ry.at[y], red_s.at[4], red_r.at[4], (f, zl * NY + yy))
    drain(ry.at[pl.ds(0, NY - 1)], red_r.at[4])
    total = s4[y]
    for e in range(1, NY):
        total = total + ry[(y + e) % NY]
    s5[...] = total
    gfin[y] = total
    for e in range(1, NY):
        yy = (y + e) % NY
        remote(s5, gfin.at[y], red_s.at[5], red_r.at[5], (f, zl * NY + yy))
    drain(ry.at[pl.ds(0, NY - 1)], red_r.at[5])
    both = gfin[...].reshape(SHARD, BLOCK)
    gd_ref[...] = both[:, :ADAPTER_RANK]
    gu_ref[...] = both[:, ADAPTER_RANK:]

    drain(dq_ref, blk_r.at[2])
    drain(dk_ref, blk_r.at[3])
    drain(dv_ref, blk_r.at[4])
    for n in range(3):
        drain(qh.at[pl.ds(0, NB - 1)], qkv_s.at[n])
    for n in range(5):
        drain(qh.at[pl.ds(0, NB - 1)], blk_s.at[n])
    drain(ab.at[0, pl.ds(0, 3), 0], abz_s.at[0])
    drain(ab.at[pl.ds(0, 3), :, 0], abz_s.at[1])
    drain(ab.at[:, :, 0], abz_s.at[2])
    drain(wfull.at[0, pl.ds(0, 3), 0], wz_s)
    drain(wfull.at[pl.ds(0, 3), :, 0], wx_s)
    drain(wfull.at[:, :, 0], wc_s)
    drain(rc, red_s.at[0])
    drain(rx.at[pl.ds(0, 3)], red_s.at[1])
    drain(rz.at[pl.ds(0, 3)], red_s.at[2])
    drain(rl, red_s.at[3])
    drain(ry.at[pl.ds(0, NY - 1)], red_s.at[4])
    drain(ry.at[pl.ds(0, NY - 1)], red_s.at[5])


def shards(q, k, v, blocks, w, a, b, cot):
    hbm = pl.BlockSpec(memory_space=pl.ANY)
    vmem = pl.BlockSpec(memory_space=pltpu.VMEM)
    smem = pl.BlockSpec(memory_space=pltpu.SMEM)
    dma = pltpu.SemaphoreType.DMA
    blocks3 = pltpu.VMEM((NB, BLOCK, BLOCK), BF16)
    tokens = jax.ShapeDtypeStruct((BLOCK, MODEL_WIDTH), BF16)
    grad = jax.ShapeDtypeStruct((SHARD, ADAPTER_RANK), F32)
    return pl.pallas_call(
        kernel,
        out_shape=(tokens, tokens, tokens, tokens, grad, grad),
        in_specs=[hbm, hbm, hbm, smem, hbm, vmem, vmem, vmem],
        out_specs=(vmem, hbm, hbm, hbm, vmem, vmem),
        scratch_shapes=[
            blocks3,
            blocks3,
            blocks3,
            blocks3,
            blocks3,
            blocks3,
            pltpu.VMEM((BLOCK, MODEL_WIDTH), BF16),
            blocks3,
            blocks3,
            blocks3,
            pltpu.VMEM((NZ, NX, 2, SHARD, MODEL_WIDTH), BF16),
            pltpu.VMEM((NZ, NX, 2, SHARD, 2 * ADAPTER_RANK), BF16),
            pltpu.VMEM((NB, KEY_BLOCKS * BLOCK, BLOCK), F32),
            pltpu.VMEM((NB, KEY_BLOCKS, BLOCK, BLOCK), BF16),
            pltpu.VMEM((NB, KEY_BLOCKS, BLOCK, BLOCK), BF16),
            pltpu.VMEM((RANDOM + 1, BLOCK, BLOCK), F32),
            pltpu.VMEM((RANDOM + 1, BLOCK, BLOCK), F32),
            pltpu.VMEM((BLOCK, 2 * ADAPTER_RANK), BF16),
            pltpu.VMEM((NZ, NX, 2, SHARD, BLOCK), F32),
            pltpu.VMEM((NZ, NX, SHARD, BLOCK), F32),
            pltpu.VMEM((NZ, NX, SHARD, BLOCK), F32),
            pltpu.VMEM((NX, NZ, SHARD, BLOCK), F32),
            pltpu.VMEM((NZ, SHARD, BLOCK), F32),
            pltpu.VMEM((NZ, SHARD, BLOCK), F32),
            pltpu.VMEM((SHARD, BLOCK), F32),
            pltpu.VMEM((SHARD, BLOCK), F32),
            pltpu.VMEM((NY, 8, BLOCK), F32),
            pltpu.VMEM((NY, 8, BLOCK), F32),
            pltpu.VMEM((8, BLOCK), F32),
            pltpu.VMEM((NY, 8, BLOCK), F32),
            pltpu.SMEM((RANDOM,), jnp.int32),
            pltpu.SMEM((RANDOM,), jnp.int32),
            pltpu.SMEM((RANDOM,), F32),
            pltpu.SMEM((NB,), jnp.int32),
            pltpu.SMEM((NB,), F32),
            dma((3,)),
            dma((3,)),
            dma((5,)),
            dma((5,)),
            dma((3,)),
            dma((3,)),
            dma,
            dma((NZ,)),
            dma,
            dma((NZ, NX)),
            dma,
            dma((NZ, NX)),
            dma,
            dma((6,)),
            dma((6,)),
        ],
        compiler_params=pltpu.CompilerParams(
            collective_id=0, has_side_effects=True, vmem_limit_bytes=60 * 2**20
        ),
    )(q, k, v, blocks, w, a, b, cot)


def solution(mesh):
    rows = P(("fsdp", "sp"), None)
    return jax.shard_map(
        shards,
        mesh=mesh,
        in_specs=(rows, rows, rows, P("fsdp", None, None), P("fsdp", None), P("fsdp", None), P("fsdp", None), rows),
        out_specs=(rows, rows, rows, rows, P("fsdp", None), P("fsdp", None)),
        check_vma=False,
    )
```

```python
import math

import jax
import jax.numpy as jnp
from jax import lax
from jax.experimental import pallas as pl
from jax.experimental.pallas import tpu as pltpu
from jax.sharding import PartitionSpec as P

MODEL_WIDTH = 2048
HEADS = 16
BLOCK = 128
KEY_BLOCKS = 6
ADAPTER_RANK = 64
TOKENS = 65536

NZ, NX = 4, 4
NL, NY = 2, 8
NB = NL * NY
SHARD = 64
RANDOM = 2 * NB

MESH = pl.DeviceIdType.MESH
F32 = jnp.float32
BF16 = jnp.bfloat16


def dot(a, b, ca, cb):
    return lax.dot_general(a, b, (((ca,), (cb,)), ((), ())), preferred_element_type=F32)


def drain(ref, sem):
    pltpu.make_async_copy(ref, ref, sem).wait()


def kernel(
    q_ref,
    k_ref,
    v_ref,
    blk,
    w_ref,
    a_ref,
    b_ref,
    cot,
    mixed_ref,
    dq_ref,
    dk_ref,
    dv_ref,
    gd_ref,
    gu_ref,
    qh,
    kh,
    vh,
    gh,
    ctx_heads,
    dctx_send,
    ctx,
    dqb,
    dkb,
    dvb,
    wfull,
    ab,
    probs,
    wts,
    dsc,
    pre_k,
    pre_v,
    d0,
    l0,
    part,
    rc,
    s1,
    rx,
    s2,
    rz,
    s3,
    rl,
    s4,
    ry,
    s5,
    gfin,
    rank,
    perm,
    same,
    last,
    has,
    qkv_s,
    qkv_r,
    blk_s,
    blk_r,
    abz_s,
    abz_r,
    wz_s,
    wz_r,
    wx_s,
    wx_r,
    wc_s,
    wc_r,
    own_sem,
    red_s,
    red_r,
):
    f = lax.axis_index("fsdp")
    j = lax.axis_index("sp")
    z, x, c = f // (2 * NX), (f // 2) % NX, f % 2
    zl, y = j // NY, j % NY
    oc = 1 - c
    scaling = 1.0 / math.sqrt(BLOCK)
    log2e = 1.4426950408889634

    def fid(zz, xx, cc):
        return zz * (2 * NX) + xx * 2 + cc

    def sp_peer(d):
        return (j + d) % NB

    sibling = (fid(z, x, oc), j)

    def xpeer(d):
        return (fid(z, (x + d) % NX, c), j)

    def zpeer(d):
        return (fid((z + d) % NZ, x, c), j)

    side = 1 - 2 * zl
    pair = (f, (1 - zl) * NY + y)
    outer = (fid((z - side + NZ) % NZ, x, c), (1 - zl) * NY + y)

    def remote(src, dst, ssem, rsem, dev):
        pltpu.make_async_remote_copy(
            src_ref=src, dst_ref=dst, send_sem=ssem, recv_sem=rsem, device_id=dev, device_id_type=MESH
        ).start()

    def cols(h):
        return pl.ds(pl.multiple_of(h * BLOCK, BLOCK), BLOCK)

    barrier = pltpu.get_barrier_semaphore()

    def greet(d, carry):
        pl.semaphore_signal(barrier, inc=1, device_id=(f, sp_peer(d)), device_id_type=MESH)
        return carry

    lax.fori_loop(1, NB, greet, 0)
    for d in (1, 2, 3):
        pl.semaphore_signal(barrier, inc=1, device_id=xpeer(d), device_id_type=MESH)
        pl.semaphore_signal(barrier, inc=1, device_id=zpeer(d), device_id_type=MESH)
    pl.semaphore_signal(barrier, inc=1, device_id=sibling, device_id_type=MESH)
    pl.semaphore_signal(barrier, inc=1, device_id=outer, device_id_type=MESH)
    pl.semaphore_wait(barrier, NB - 1 + 8)

    ab[z, x, c] = jnp.concatenate([a_ref[...], b_ref[...]], axis=1)
    for d in (1, 3, 2):
        remote(ab.at[z, x, c], ab.at[z, x, c], abz_s.at[0], abz_r.at[0], zpeer(d))

    for n, (src, dst) in enumerate(((k_ref, kh), (q_ref, qh), (v_ref, vh))):

        def send_heads(d, carry, src=src, dst=dst, n=n):
            h = sp_peer(d)
            remote(src.at[:, cols(h)], dst.at[j], qkv_s.at[n], qkv_r.at[n], (f, h))
            return carry

        lax.fori_loop(1, NB, send_heads, 0)
        pltpu.make_async_copy(src.at[:, cols(j)], dst.at[j], qkv_r.at[n]).start()
        if n == 0:
            remote(w_ref, wfull.at[z, x, c], wz_s, wz_r.at[z], outer)
            pltpu.make_async_copy(w_ref, wfull.at[z, x, c], own_sem).start()
            remote(w_ref, wfull.at[z, x, c], wc_s, wc_r.at[z, x], sibling)
            drain(ab.at[0, pl.ds(0, 3), 0], abz_r.at[0])
            for d in (1, 3, 2):
                remote(ab.at[:, x, c], ab.at[:, x, c], abz_s.at[1], abz_r.at[1], xpeer(d))
            for d in (1, 3):
                remote(w_ref, wfull.at[z, x, c], wx_s, wx_r.at[z, x], xpeer(d))

    def entry(r):
        return blk[4 + r % 2, 0, r // 2]

    def rank_of(r, carry):
        mine = entry(r) * RANDOM + r
        total = jnp.int32(0)
        for s in range(RANDOM):
            total = total + jnp.where(entry(s) * RANDOM + s < mine, 1, 0)
        rank[r] = total
        return carry

    lax.fori_loop(0, RANDOM, rank_of, 0)

    def perm_of(p, carry):
        total = jnp.int32(0)
        for s in range(RANDOM):
            total = total + jnp.where(rank[s] == p, s, 0)
        perm[p] = total
        named = blk[4 + total % 2, 0, total // 2]
        same[p] = jnp.where(named == carry, 1.0, 0.0).astype(F32)
        return named

    lax.fori_loop(0, RANDOM, perm_of, jnp.int32(-1))

    def last_of(n, carry):
        upto = jnp.int32(0)
        equal = jnp.int32(0)
        for s in range(RANDOM):
            upto = upto + jnp.where(entry(s) <= n, 1, 0)
            equal = equal + jnp.where(entry(s) == n, 1, 0)
        last[n] = jnp.maximum(upto - 1, 0)
        has[n] = jnp.where(equal > 0, 1.0, 0.0).astype(F32)
        return carry

    lax.fori_loop(0, NB, last_of, 0)

    drain(ab.at[pl.ds(0, 3), :, 0], abz_r.at[1])
    remote(ab.at[:, :, c], ab.at[:, :, c], abz_s.at[2], abz_r.at[2], sibling)

    mine, near, next_, far = z, (z - side + NZ) % NZ, (z + side + NZ) % NZ, (z + 2) % NZ
    left, right = (x + NX - 1) % NX, (x + 1) % NX
    half = SHARD // 2

    def forward_z(u, onward):
        piece = wfull.at[u, x, c]
        drain(piece, wz_r.at[u])
        if onward is not None:
            remote(piece, piece, wz_s, wz_r.at[u], onward)
        for e in (1, 3):
            remote(piece, piece, wx_s, wx_r.at[u, x], xpeer(e))
        remote(piece, piece, wc_s, wc_r.at[u, x], sibling)

    def forward_x(u):
        for xx, start, e in ((left, 0, 1), (right, half, 3)):
            piece = wfull.at[u, xx, c]
            drain(piece, wx_r.at[u, xx])
            part_ = wfull.at[u, xx, c, pl.ds(start, half)]
            remote(part_, part_, wx_s, wx_r.at[u, xx], xpeer(e))
            remote(piece, piece, wc_s, wc_r.at[u, xx], sibling)

    def forward_last(u):
        xx = (x + 2) % NX
        piece = wfull.at[u, xx, c]
        drain(piece, wx_r.at[u, xx])
        remote(piece, piece, wc_s, wc_r.at[u, xx], sibling)

    def context_gradient(u):
        def one_head(e, carry):
            xx = (x + e) % NX
            h = u * NX + xx
            drain(wfull.at[u, xx, oc], wc_r.at[u, xx])
            rows = wfull[u, xx].reshape(BLOCK, MODEL_WIDTH)
            adapter = ab[u, xx].reshape(BLOCK, 2 * ADAPTER_RANK)
            g = dot(cot[...], rows, 1, 1) + dot(d0[...], adapter, 1, 1)
            dctx_send[h] = g.astype(BF16)

            @pl.when(h != j)
            def _():
                remote(dctx_send.at[h], gh.at[j], blk_s.at[1], blk_r.at[1], (f, h))

            @pl.when(h == j)
            def _():
                pltpu.make_async_copy(dctx_send.at[h], gh.at[j], blk_r.at[1]).start()

            return carry

        lax.fori_loop(0, NX, one_head, 0)

    forward_z(near, pair)
    forward_x(mine)
    forward_z(next_, outer)
    forward_last(mine)

    drain(w_ref, own_sem)
    drain(ab.at[:, :, 0], abz_r.at[2])
    lane = lax.broadcasted_iota(jnp.int32, (BLOCK, 2 * ADAPTER_RANK), 1)
    both = dot(cot[...], ab[...].reshape(MODEL_WIDTH, 2 * ADAPTER_RANK), 1, 0)
    d0[...] = jnp.where(lane < ADAPTER_RANK, pltpu.roll(both, ADAPTER_RANK, 1), 0.0).astype(BF16)

    context_gradient(mine)
    forward_x(near)
    forward_z(far, None)
    forward_last(near)
    context_gradient(near)
    forward_x(next_)
    forward_last(next_)
    context_gradient(next_)
    forward_x(far)

    drain(kh, qkv_r.at[0])
    drain(qh, qkv_r.at[1])
    drain(vh, qkv_r.at[2])

    def gathered(ref, i):
        return jnp.concatenate([ref[blk[s, 0, i]] for s in range(KEY_BLOCKS)], axis=0)

    def send_block(src, dst_ref, n, i):
        @pl.when(i != j)
        def _():
            remote(src.at[i], dst_ref.at[:, cols(j)], blk_s.at[n], blk_r.at[n], (f, i))

        @pl.when(i == j)
        def _():
            pltpu.make_async_copy(src.at[i], dst_ref.at[:, cols(j)], blk_r.at[n]).start()

    def forward_block(t, carry):
        i = sp_peer(t)
        scores = dot(gathered(kh, i), qh[i], 1, 1)
        highest = jnp.max(scores, axis=0, keepdims=True)
        raised = jnp.exp2((scores - highest) * (scaling * log2e))
        p = raised * (1.0 / jnp.sum(raised, axis=0, keepdims=True))
        probs[i] = p
        w = p.astype(BF16)
        wts[i] = w.reshape(KEY_BLOCKS, BLOCK, BLOCK)
        ctx_heads[i] = dot(w, gathered(vh, i), 0, 0).astype(BF16)
        send_block(ctx_heads, ctx, 0, i)
        return carry

    lax.fori_loop(1, NB + 1, forward_block, 0, unroll=2)

    forward_last(far)
    context_gradient(far)

    drain(ctx, blk_r.at[0])
    both = dot(ctx[...], ab[...].reshape(MODEL_WIDTH, 2 * ADAPTER_RANK), 1, 0)
    low = jnp.where(lane >= ADAPTER_RANK, pltpu.roll(both, ADAPTER_RANK, 1), 0.0).astype(BF16)
    l0[...] = low
    normal = 1.0 / math.sqrt(TOKENS)

    def partial(h, carry):
        s = dot(ctx[:, cols(h)], d0[...], 0, 0) + dot(cot[:, cols(h)], l0[...], 0, 0)
        part[h // NX, h % NX] = (s * normal).reshape(2, SHARD, BLOCK)
        return carry

    lax.fori_loop(0, HEADS, partial, 0, unroll=2)
    remote(part.at[:, :, oc], rc, red_s.at[0], red_r.at[0], sibling)

    drain(gh, blk_r.at[1])

    def backward_block(t, carry):
        i = sp_peer(t)
        p = probs[i]
        dw = dot(gathered(vh, i), gh[i], 1, 1)
        correction = jnp.sum(p * dw, axis=0, keepdims=True)
        ds = (p * (dw - correction) * scaling).astype(BF16)
        dsc[i] = ds.reshape(KEY_BLOCKS, BLOCK, BLOCK)
        dqb[i] = dot(ds, gathered(kh, i), 0, 0).astype(BF16)
        send_block(dqb, dq_ref, 2, i)
        return carry

    lax.fori_loop(1, NB + 1, backward_block, 0, unroll=2)

    drain(rc, red_r.at[0])

    def add_core(u, carry):
        s1[u] = part[u, :, c] + rc[u]
        return carry

    lax.fori_loop(0, NZ, add_core, 0)
    for e in (1, 3, 2):
        remote(s1.at[:, (x + e) % NX], rx.at[x], red_s.at[1], red_r.at[1], xpeer(e))

    def random_terms(p, carry):
        r = perm[p]
        i = r // 2
        slot = 4 + r % 2
        keep = same[p]
        acc_k = carry[0] * keep + dot(dsc[i, slot], qh[i], 1, 0)
        acc_v = carry[1] * keep + dot(wts[i, slot], gh[i], 1, 0)
        pre_k[p] = acc_k
        pre_v[p] = acc_v
        return acc_k, acc_v

    zero = jnp.zeros((BLOCK, BLOCK), F32)
    lax.fori_loop(0, RANDOM, random_terms, (zero, zero), unroll=4)

    def long_dot(terms, rows):
        wide = jnp.concatenate(terms, axis=1)
        return dot(wide, jnp.concatenate(rows, axis=0), 1, 0)

    every = range(NB)
    pre_k[RANDOM] = long_dot([dsc[i, 3] for i in every], [qh[i] for i in every])
    pre_v[RANDOM] = long_dot([wts[i, 3] for i in every], [gh[i] for i in every])
    common = blk[3, 0, 0]

    def key_block(t, carry):
        n = sp_peer(t)
        before, after = (n + NB - 1) % NB, (n + 1) % NB
        slot_before = jnp.where(blk[2, 0, before] == n, 2, 0)
        slot_after = jnp.where(blk[0, 0, after] == n, 0, 2)
        is_common = jnp.where(common == n, 1.0, 0.0).astype(F32)

        def total(terms, rows, pre):
            window = long_dot(
                [terms[n, 1], terms[before, slot_before], terms[after, slot_after]],
                [rows[n], rows[before], rows[after]],
            )
            return (window + pre[last[n]] * has[n] + pre[RANDOM] * is_common).astype(BF16)

        dkb[n] = total(dsc, qh, pre_k)
        send_block(dkb, dk_ref, 3, n)
        dvb[n] = total(wts, gh, pre_v)
        send_block(dvb, dv_ref, 4, n)
        return carry

    lax.fori_loop(1, NB + 1, key_block, 0)

    drain(rx.at[pl.ds(0, 3)], red_r.at[1])
    s2[...] = s1[:, x] + rx[(x + 1) % NX] + rx[(x + 2) % NX] + rx[(x + 3) % NX]
    for e in (1, 3, 2):
        remote(s2.at[(z + e) % NZ], rz.at[z], red_s.at[2], red_r.at[2], zpeer(e))

    wide = 256

    def output_columns(n, carry):
        rows = wfull[:, :, :, :, pl.ds(pl.multiple_of(n * wide, wide), wide)]
        adapter = ab[n // 2, pl.ds(2 * (n % 2), 2)].reshape(wide, 2 * ADAPTER_RANK)
        m = dot(ctx[...], rows.reshape(MODEL_WIDTH, wide), 1, 0) + dot(l0[...], adapter, 1, 1)
        mixed_ref[:, pl.ds(pl.multiple_of(n * wide, wide), wide)] = m.astype(BF16)
        return carry

    lax.fori_loop(0, MODEL_WIDTH // wide, output_columns, 0)

    drain(rz.at[pl.ds(0, 3)], red_r.at[2])
    s3[...] = s2[z] + rz[(z + 1) % NZ] + rz[(z + 2) % NZ] + rz[(z + 3) % NZ]
    remote(s3, rl, red_s.at[3], red_r.at[3], (f, (1 - zl) * NY + y))
    drain(rl, red_r.at[3])
    s4[...] = (s3[...] + rl[...]).reshape(NY, 8, BLOCK)
    for e in range(1, NY):
        yy = (y + e) % NY
        remote(s4.at[yy], ry.at[y], red_s.at[4], red_r.at[4], (f, zl * NY + yy))
    drain(ry.at[pl.ds(0, NY - 1)], red_r.at[4])
    total = s4[y]
    for e in range(1, NY):
        total = total + ry[(y + e) % NY]
    s5[...] = total
    gfin[y] = total
    for e in range(1, NY):
        yy = (y + e) % NY
        remote(s5, gfin.at[y], red_s.at[5], red_r.at[5], (f, zl * NY + yy))
    drain(ry.at[pl.ds(0, NY - 1)], red_r.at[5])
    both = gfin[...].reshape(SHARD, BLOCK)
    gd_ref[...] = both[:, :ADAPTER_RANK]
    gu_ref[...] = both[:, ADAPTER_RANK:]

    drain(dq_ref, blk_r.at[2])
    drain(dk_ref, blk_r.at[3])
    drain(dv_ref, blk_r.at[4])
    for n in range(3):
        drain(qh.at[pl.ds(0, NB - 1)], qkv_s.at[n])
    for n in range(5):
        drain(qh.at[pl.ds(0, NB - 1)], blk_s.at[n])
    drain(ab.at[0, pl.ds(0, 3), 0], abz_s.at[0])
    drain(ab.at[pl.ds(0, 3), :, 0], abz_s.at[1])
    drain(ab.at[:, :, 0], abz_s.at[2])
    drain(wfull.at[0, pl.ds(0, 3), 0], wz_s)
    drain(wfull.at[pl.ds(0, 3), :, 0], wx_s)
    drain(wfull.at[:, :, 0], wc_s)
    drain(rc, red_s.at[0])
    drain(rx.at[pl.ds(0, 3)], red_s.at[1])
    drain(rz.at[pl.ds(0, 3)], red_s.at[2])
    drain(rl, red_s.at[3])
    drain(ry.at[pl.ds(0, NY - 1)], red_s.at[4])
    drain(ry.at[pl.ds(0, NY - 1)], red_s.at[5])


def copy_out(*refs):
    n = len(refs) // 2
    for source, target in zip(refs[:n], refs[n:]):
        target[...] = source[...]


def shards(q, k, v, blocks, w, a, b, cot):
    hbm = pl.BlockSpec(memory_space=pl.ANY)
    vmem = pl.BlockSpec(memory_space=pltpu.VMEM)
    smem = pl.BlockSpec(memory_space=pltpu.SMEM)
    dma = pltpu.SemaphoreType.DMA
    blocks3 = pltpu.VMEM((NB, BLOCK, BLOCK), BF16)
    tokens = jax.ShapeDtypeStruct((BLOCK, MODEL_WIDTH), BF16)
    grad = jax.ShapeDtypeStruct((SHARD, ADAPTER_RANK), F32)
    outs = pl.pallas_call(
        kernel,
        out_shape=(tokens, tokens, tokens, tokens, grad, grad),
        in_specs=[hbm, hbm, hbm, smem, hbm, vmem, vmem, vmem],
        out_specs=(vmem, hbm, hbm, hbm, vmem, vmem),
        scratch_shapes=[
            blocks3,
            blocks3,
            blocks3,
            blocks3,
            blocks3,
            blocks3,
            pltpu.VMEM((BLOCK, MODEL_WIDTH), BF16),
            blocks3,
            blocks3,
            blocks3,
            pltpu.VMEM((NZ, NX, 2, SHARD, MODEL_WIDTH), BF16),
            pltpu.VMEM((NZ, NX, 2, SHARD, 2 * ADAPTER_RANK), BF16),
            pltpu.VMEM((NB, KEY_BLOCKS * BLOCK, BLOCK), F32),
            pltpu.VMEM((NB, KEY_BLOCKS, BLOCK, BLOCK), BF16),
            pltpu.VMEM((NB, KEY_BLOCKS, BLOCK, BLOCK), BF16),
            pltpu.VMEM((RANDOM + 1, BLOCK, BLOCK), F32),
            pltpu.VMEM((RANDOM + 1, BLOCK, BLOCK), F32),
            pltpu.VMEM((BLOCK, 2 * ADAPTER_RANK), BF16),
            pltpu.VMEM((BLOCK, 2 * ADAPTER_RANK), BF16),
            pltpu.VMEM((NZ, NX, 2, SHARD, BLOCK), F32),
            pltpu.VMEM((NZ, NX, SHARD, BLOCK), F32),
            pltpu.VMEM((NZ, NX, SHARD, BLOCK), F32),
            pltpu.VMEM((NX, NZ, SHARD, BLOCK), F32),
            pltpu.VMEM((NZ, SHARD, BLOCK), F32),
            pltpu.VMEM((NZ, SHARD, BLOCK), F32),
            pltpu.VMEM((SHARD, BLOCK), F32),
            pltpu.VMEM((SHARD, BLOCK), F32),
            pltpu.VMEM((NY, 8, BLOCK), F32),
            pltpu.VMEM((NY, 8, BLOCK), F32),
            pltpu.VMEM((8, BLOCK), F32),
            pltpu.VMEM((NY, 8, BLOCK), F32),
            pltpu.SMEM((RANDOM,), jnp.int32),
            pltpu.SMEM((RANDOM,), jnp.int32),
            pltpu.SMEM((RANDOM,), F32),
            pltpu.SMEM((NB,), jnp.int32),
            pltpu.SMEM((NB,), F32),
            dma((3,)),
            dma((3,)),
            dma((5,)),
            dma((5,)),
            dma((3,)),
            dma((3,)),
            dma,
            dma((NZ,)),
            dma,
            dma((NZ, NX)),
            dma,
            dma((NZ, NX)),
            dma,
            dma((6,)),
            dma((6,)),
        ],
        compiler_params=pltpu.CompilerParams(
            collective_id=0, has_side_effects=True, vmem_limit_bytes=60 * 2**20
        ),
    )(q, k, v, jnp.transpose(blocks, (2, 0, 1)), w, a, b, cot)
    steps = 4
    pieces = [pl.BlockSpec((o.shape[0] // steps, o.shape[1]), lambda i: (i, 0)) for o in outs]
    return pl.pallas_call(
        copy_out,
        out_shape=tuple(jax.ShapeDtypeStruct(o.shape, o.dtype) for o in outs),
        grid=(steps,),
        in_specs=pieces,
        out_specs=tuple(pieces),
    )(*outs)


def solution(mesh):
    rows = P(("fsdp", "sp"), None)
    return jax.shard_map(
        shards,
        mesh=mesh,
        in_specs=(rows, rows, rows, P("fsdp", None, None), P("fsdp", None), P("fsdp", None), P("fsdp", None), rows),
        out_specs=(rows, rows, rows, rows, P("fsdp", None), P("fsdp", None)),
        check_vma=False,
    )
```

```python
import math

import jax
import jax.numpy as jnp
from jax import lax
from jax.experimental import pallas as pl
from jax.experimental.pallas import tpu as pltpu
from jax.sharding import PartitionSpec as P

MODEL_WIDTH = 2048
HEADS = 16
BLOCK = 128
KEY_BLOCKS = 6
ADAPTER_RANK = 64
TOKENS = 65536

NZ, NX = 4, 4
NL, NY = 2, 8
NB = NL * NY
SHARD = 64
RANDOM = 2 * NB

MESH = pl.DeviceIdType.MESH
F32 = jnp.float32
BF16 = jnp.bfloat16


def dot(a, b, ca, cb):
    return lax.dot_general(a, b, (((ca,), (cb,)), ((), ())), preferred_element_type=F32)


def drain(ref, sem):
    pltpu.make_async_copy(ref, ref, sem).wait()


def kernel(
    q_ref,
    k_ref,
    v_ref,
    blk,
    w_ref,
    a_ref,
    b_ref,
    cot,
    mixed_ref,
    dq_ref,
    dk_ref,
    dv_ref,
    gd_ref,
    gu_ref,
    qh,
    kh,
    vh,
    gh,
    ctx_heads,
    dctx_send,
    ctx,
    dqb,
    dkb,
    dvb,
    wfull,
    ab,
    probs,
    wts,
    dsc,
    pre_k,
    pre_v,
    d0,
    l0,
    part,
    rc,
    s1,
    rx,
    s2,
    rz,
    s3,
    rl,
    s4,
    ry,
    s5,
    gfin,
    rank,
    perm,
    same,
    last,
    has,
    qkv_s,
    qkv_r,
    blk_s,
    blk_r,
    abz_s,
    abz_r,
    wz_s,
    wz_r,
    wx_s,
    wx_r,
    wc_s,
    wc_r,
    own_sem,
    red_s,
    red_r,
):
    f = lax.axis_index("fsdp")
    j = lax.axis_index("sp")
    z, x, c = f // (2 * NX), (f // 2) % NX, f % 2
    zl, y = j // NY, j % NY
    oc = 1 - c
    scaling = 1.0 / math.sqrt(BLOCK)
    log2e = 1.4426950408889634

    def fid(zz, xx, cc):
        return zz * (2 * NX) + xx * 2 + cc

    def sp_peer(d):
        return (j + d) % NB

    def peer(t):
        k = t // NL
        away = NY // 2 + (1 - 2 * (k % 2)) * ((k + 1) // 2)
        return ((zl + t % NL) % NL) * NY + (y + away) % NY

    sibling = (fid(z, x, oc), j)

    def xpeer(d):
        return (fid(z, (x + d) % NX, c), j)

    def zpeer(d):
        return (fid((z + d) % NZ, x, c), j)

    side = 1 - 2 * zl
    pair = (f, (1 - zl) * NY + y)
    outer = (fid((z - side + NZ) % NZ, x, c), (1 - zl) * NY + y)

    def remote(src, dst, ssem, rsem, dev):
        pltpu.make_async_remote_copy(
            src_ref=src, dst_ref=dst, send_sem=ssem, recv_sem=rsem, device_id=dev, device_id_type=MESH
        ).start()

    def cols(h):
        return pl.ds(pl.multiple_of(h * BLOCK, BLOCK), BLOCK)

    barrier = pltpu.get_barrier_semaphore()

    def greet(d, carry):
        pl.semaphore_signal(barrier, inc=1, device_id=(f, sp_peer(d)), device_id_type=MESH)
        return carry

    lax.fori_loop(1, NB, greet, 0)
    for d in (1, 2, 3):
        pl.semaphore_signal(barrier, inc=1, device_id=xpeer(d), device_id_type=MESH)
        pl.semaphore_signal(barrier, inc=1, device_id=zpeer(d), device_id_type=MESH)
    pl.semaphore_signal(barrier, inc=1, device_id=sibling, device_id_type=MESH)
    pl.semaphore_signal(barrier, inc=1, device_id=outer, device_id_type=MESH)
    pl.semaphore_wait(barrier, NB - 1 + 8)

    ab[z, x, c] = jnp.concatenate([a_ref[...], b_ref[...]], axis=1)
    for d in (1, 3, 2):
        remote(ab.at[z, x, c], ab.at[z, x, c], abz_s.at[0], abz_r.at[0], zpeer(d))

    for n, (src, dst) in enumerate(((k_ref, kh), (q_ref, qh), (v_ref, vh))):

        def send_heads(t, carry, src=src, dst=dst, n=n):
            h = peer(t + t // (NB - 2))
            remote(src.at[:, cols(h)], dst.at[j], qkv_s.at[n], qkv_r.at[n], (f, h))
            return carry

        lax.fori_loop(0, NB - 1, send_heads, 0)
        pltpu.make_async_copy(src.at[:, cols(j)], dst.at[j], qkv_r.at[n]).start()
        if n == 0:
            remote(w_ref, wfull.at[z, x, c], wz_s, wz_r.at[z], outer)
            pltpu.make_async_copy(w_ref, wfull.at[z, x, c], own_sem).start()
            remote(w_ref, wfull.at[z, x, c], wc_s, wc_r.at[z, x], sibling)
            drain(ab.at[0, pl.ds(0, 3), 0], abz_r.at[0])
            for d in (1, 3, 2):
                remote(ab.at[:, x, c], ab.at[:, x, c], abz_s.at[1], abz_r.at[1], xpeer(d))
            for d in (1, 3):
                remote(w_ref, wfull.at[z, x, c], wx_s, wx_r.at[z, x], xpeer(d))

    def entry(r):
        return blk[4 + r % 2, 0, r // 2]

    def rank_of(r, carry):
        mine = entry(r) * RANDOM + r
        total = jnp.int32(0)
        for s in range(RANDOM):
            total = total + jnp.where(entry(s) * RANDOM + s < mine, 1, 0)
        rank[r] = total
        return carry

    lax.fori_loop(0, RANDOM, rank_of, 0)

    def perm_of(p, carry):
        total = jnp.int32(0)
        for s in range(RANDOM):
            total = total + jnp.where(rank[s] == p, s, 0)
        perm[p] = total
        named = blk[4 + total % 2, 0, total // 2]
        same[p] = jnp.where(named == carry, 1.0, 0.0).astype(F32)
        return named

    lax.fori_loop(0, RANDOM, perm_of, jnp.int32(-1))

    def last_of(n, carry):
        upto = jnp.int32(0)
        equal = jnp.int32(0)
        for s in range(RANDOM):
            upto = upto + jnp.where(entry(s) <= n, 1, 0)
            equal = equal + jnp.where(entry(s) == n, 1, 0)
        last[n] = jnp.maximum(upto - 1, 0)
        has[n] = jnp.where(equal > 0, 1.0, 0.0).astype(F32)
        return carry

    lax.fori_loop(0, NB, last_of, 0)

    drain(ab.at[pl.ds(0, 3), :, 0], abz_r.at[1])
    remote(ab.at[:, :, c], ab.at[:, :, c], abz_s.at[2], abz_r.at[2], sibling)

    mine, near, next_, far = z, (z - side + NZ) % NZ, (z + side + NZ) % NZ, (z + 2) % NZ
    left, right = (x + NX - 1) % NX, (x + 1) % NX
    half = SHARD // 2

    def forward_z(u, onward):
        piece = wfull.at[u, x, c]
        drain(piece, wz_r.at[u])
        if onward is not None:
            remote(piece, piece, wz_s, wz_r.at[u], onward)
        for e in (1, 3):
            remote(piece, piece, wx_s, wx_r.at[u, x], xpeer(e))
        remote(piece, piece, wc_s, wc_r.at[u, x], sibling)

    def forward_x(u):
        for xx, start, e in ((left, 0, 1), (right, half, 3)):
            piece = wfull.at[u, xx, c]
            drain(piece, wx_r.at[u, xx])
            part_ = wfull.at[u, xx, c, pl.ds(start, half)]
            remote(part_, part_, wx_s, wx_r.at[u, xx], xpeer(e))
            remote(piece, piece, wc_s, wc_r.at[u, xx], sibling)

    def forward_last(u):
        xx = (x + 2) % NX
        piece = wfull.at[u, xx, c]
        drain(piece, wx_r.at[u, xx])
        remote(piece, piece, wc_s, wc_r.at[u, xx], sibling)

    forward_z(near, pair)
    forward_x(mine)
    forward_z(next_, outer)
    forward_last(mine)

    drain(w_ref, own_sem)
    drain(ab.at[:, :, 0], abz_r.at[2])
    lane = lax.broadcasted_iota(jnp.int32, (BLOCK, 2 * ADAPTER_RANK), 1)
    both = dot(cot[...], ab[...].reshape(MODEL_WIDTH, 2 * ADAPTER_RANK), 1, 0)
    d0[...] = jnp.where(lane < ADAPTER_RANK, pltpu.roll(both, ADAPTER_RANK, 1), 0.0).astype(BF16)

    forward_x(near)
    forward_z(far, None)
    forward_last(near)
    forward_x(next_)
    forward_last(next_)
    forward_x(far)

    drain(kh, qkv_r.at[0])
    drain(qh, qkv_r.at[1])
    drain(vh, qkv_r.at[2])

    def gathered(ref, i):
        return jnp.concatenate([ref[blk[s, 0, i]] for s in range(KEY_BLOCKS)], axis=0)

    def send_block(src, dst_ref, n, i):
        @pl.when(i != j)
        def _():
            remote(src.at[i], dst_ref.at[:, cols(j)], blk_s.at[n], blk_r.at[n], (f, i))

        @pl.when(i == j)
        def _():
            pltpu.make_async_copy(src.at[i], dst_ref.at[:, cols(j)], blk_r.at[n]).start()

    def forward_block(t, carry):
        i = peer(t)
        scores = dot(gathered(kh, i), qh[i], 1, 1)
        highest = jnp.max(scores, axis=0, keepdims=True)
        raised = jnp.exp2((scores - highest) * (scaling * log2e))
        p = raised * (1.0 / jnp.sum(raised, axis=0, keepdims=True))
        probs[i] = p
        w = p.astype(BF16)
        wts[i] = w.reshape(KEY_BLOCKS, BLOCK, BLOCK)
        ctx_heads[i] = dot(w, gathered(vh, i), 0, 0).astype(BF16)
        send_block(ctx_heads, ctx, 0, i)
        return carry

    lax.fori_loop(0, NB, forward_block, 0, unroll=2)

    forward_last(far)

    def context_gradient(t, carry):
        h = peer(t)
        u, xx = h // NX, h % NX
        drain(wfull.at[u, xx, oc], wc_r.at[u, xx])
        rows = wfull[u, xx].reshape(BLOCK, MODEL_WIDTH)
        adapter = ab[u, xx].reshape(BLOCK, 2 * ADAPTER_RANK)
        g = dot(cot[...], rows, 1, 1) + dot(d0[...], adapter, 1, 1)
        dctx_send[h] = g.astype(BF16)

        @pl.when(h != j)
        def _():
            remote(dctx_send.at[h], gh.at[j], blk_s.at[1], blk_r.at[1], (f, h))

        @pl.when(h == j)
        def _():
            pltpu.make_async_copy(dctx_send.at[h], gh.at[j], blk_r.at[1]).start()

        return carry

    lax.fori_loop(0, NB, context_gradient, 0, unroll=2)

    drain(ctx, blk_r.at[0])
    both = dot(ctx[...], ab[...].reshape(MODEL_WIDTH, 2 * ADAPTER_RANK), 1, 0)
    low = jnp.where(lane >= ADAPTER_RANK, pltpu.roll(both, ADAPTER_RANK, 1), 0.0).astype(BF16)
    l0[...] = low
    normal = 1.0 / math.sqrt(TOKENS)

    def partial(h, carry):
        s = dot(ctx[:, cols(h)], d0[...], 0, 0) + dot(cot[:, cols(h)], l0[...], 0, 0)
        part[h // NX, h % NX] = (s * normal).reshape(2, SHARD, BLOCK)
        return carry

    lax.fori_loop(0, HEADS, partial, 0, unroll=2)
    remote(part.at[:, :, oc], rc, red_s.at[0], red_r.at[0], sibling)

    drain(rc, red_r.at[0])

    def add_core(u, carry):
        s1[u] = part[u, :, c] + rc[u]
        return carry

    lax.fori_loop(0, NZ, add_core, 0)
    for e in (1, 3, 2):
        remote(s1.at[:, (x + e) % NX], rx.at[x], red_s.at[1], red_r.at[1], xpeer(e))

    drain(gh, blk_r.at[1])

    def backward_block(t, carry):
        i = peer(t)
        p = probs[i]
        dw = dot(gathered(vh, i), gh[i], 1, 1)
        correction = jnp.sum(p * dw, axis=0, keepdims=True)
        ds = (p * (dw - correction) * scaling).astype(BF16)
        dsc[i] = ds.reshape(KEY_BLOCKS, BLOCK, BLOCK)
        dqb[i] = dot(ds, gathered(kh, i), 0, 0).astype(BF16)
        send_block(dqb, dq_ref, 2, i)
        return carry

    lax.fori_loop(0, NB, backward_block, 0, unroll=2)

    drain(rx.at[pl.ds(0, 3)], red_r.at[1])
    s2[...] = s1[:, x] + rx[(x + 1) % NX] + rx[(x + 2) % NX] + rx[(x + 3) % NX]
    for e in (1, 3, 2):
        remote(s2.at[(z + e) % NZ], rz.at[z], red_s.at[2], red_r.at[2], zpeer(e))

    zero = jnp.zeros((BLOCK, BLOCK), F32)
    common = blk[3, 0, 0]

    def long_dot(terms, rows):
        wide = jnp.concatenate(terms, axis=1)
        return dot(wide, jnp.concatenate(rows, axis=0), 1, 0)

    def listed_terms(terms, rows, pre):
        def random_terms(p, carry):
            r = perm[p]
            i = r // 2
            slot = 4 + r % 2
            acc = carry * same[p] + dot(terms[i, slot], rows[i], 1, 0)
            pre[p] = acc
            return acc

        lax.fori_loop(0, RANDOM, random_terms, zero, unroll=4)
        pre[RANDOM] = long_dot([terms[i, 3] for i in range(NB)], [rows[i] for i in range(NB)])

    def key_blocks(terms, rows, pre, out, out_ref, slot):
        def key_block(t, carry):
            n = peer(t)
            before, after = (n + NB - 1) % NB, (n + 1) % NB
            slot_before = jnp.where(blk[2, 0, before] == n, 2, 0)
            slot_after = jnp.where(blk[0, 0, after] == n, 0, 2)
            is_common = jnp.where(common == n, 1.0, 0.0).astype(F32)
            window = long_dot(
                [terms[n, 1], terms[before, slot_before], terms[after, slot_after]],
                [rows[n], rows[before], rows[after]],
            )
            out[n] = (window + pre[last[n]] * has[n] + pre[RANDOM] * is_common).astype(BF16)
            send_block(out, out_ref, slot, n)
            return carry

        lax.fori_loop(0, NB, key_block, 0, unroll=2)

    listed_terms(wts, gh, pre_v)
    drain(rz.at[pl.ds(0, 3)], red_r.at[2])
    s3[...] = s2[z] + rz[(z + 1) % NZ] + rz[(z + 2) % NZ] + rz[(z + 3) % NZ]
    remote(s3, rl, red_s.at[3], red_r.at[3], pair)
    key_blocks(wts, gh, pre_v, dvb, dv_ref, 4)
    listed_terms(dsc, qh, pre_k)
    drain(rl, red_r.at[3])
    s4[...] = (s3[...] + rl[...]).reshape(NY, 8, BLOCK)
    for e in range(1, NY):
        yy = (y + e) % NY
        remote(s4.at[yy], ry.at[y], red_s.at[4], red_r.at[4], (f, zl * NY + yy))
    key_blocks(dsc, qh, pre_k, dkb, dk_ref, 3)

    wide = 256

    def output_columns(n, carry):
        rows = wfull[:, :, :, :, pl.ds(pl.multiple_of(n * wide, wide), wide)]
        adapter = ab[n // 2, pl.ds(2 * (n % 2), 2)].reshape(wide, 2 * ADAPTER_RANK)
        m = dot(ctx[...], rows.reshape(MODEL_WIDTH, wide), 1, 0) + dot(l0[...], adapter, 1, 1)
        mixed_ref[:, pl.ds(pl.multiple_of(n * wide, wide), wide)] = m.astype(BF16)
        return carry

    lax.fori_loop(0, MODEL_WIDTH // wide, output_columns, 0)
    drain(ry.at[pl.ds(0, NY - 1)], red_r.at[4])
    total = s4[y]
    for e in range(1, NY):
        total = total + ry[(y + e) % NY]
    s5[...] = total
    gfin[y] = total
    for e in range(1, NY):
        yy = (y + e) % NY
        remote(s5, gfin.at[y], red_s.at[5], red_r.at[5], (f, zl * NY + yy))

    drain(ry.at[pl.ds(0, NY - 1)], red_r.at[5])
    both = gfin[...].reshape(SHARD, BLOCK)
    gd_ref[...] = both[:, :ADAPTER_RANK]
    gu_ref[...] = both[:, ADAPTER_RANK:]

    drain(dq_ref, blk_r.at[2])
    drain(dk_ref, blk_r.at[3])
    drain(dv_ref, blk_r.at[4])
    for n in range(3):
        drain(qh.at[pl.ds(0, NB - 1)], qkv_s.at[n])
    for n in range(5):
        drain(qh.at[pl.ds(0, NB - 1)], blk_s.at[n])
    drain(ab.at[0, pl.ds(0, 3), 0], abz_s.at[0])
    drain(ab.at[pl.ds(0, 3), :, 0], abz_s.at[1])
    drain(ab.at[:, :, 0], abz_s.at[2])
    drain(wfull.at[0, pl.ds(0, 3), 0], wz_s)
    drain(wfull.at[pl.ds(0, 3), :, 0], wx_s)
    drain(wfull.at[:, :, 0], wc_s)
    drain(rc, red_s.at[0])
    drain(rx.at[pl.ds(0, 3)], red_s.at[1])
    drain(rz.at[pl.ds(0, 3)], red_s.at[2])
    drain(rl, red_s.at[3])
    drain(ry.at[pl.ds(0, NY - 1)], red_s.at[4])
    drain(ry.at[pl.ds(0, NY - 1)], red_s.at[5])


def copy_out(*refs):
    n = (len(refs) - 2) // 3
    sources, targets, held = refs[:n], refs[n : 2 * n], refs[2 * n : 3 * n]
    in_sem, out_sem = refs[3 * n :]
    inward = [pltpu.make_async_copy(sources[i], held[i], in_sem.at[i]) for i in range(n)]
    outward = [pltpu.make_async_copy(held[i], targets[i], out_sem.at[i]) for i in range(n)]
    for copy in inward:
        copy.start()
    for i in range(n):
        inward[i].wait()
        outward[i].start()
    for copy in outward:
        copy.wait()


def shards(q, k, v, blocks, w, a, b, cot):
    hbm = pl.BlockSpec(memory_space=pl.ANY)
    vmem = pl.BlockSpec(memory_space=pltpu.VMEM)
    smem = pl.BlockSpec(memory_space=pltpu.SMEM)
    dma = pltpu.SemaphoreType.DMA
    blocks3 = pltpu.VMEM((NB, BLOCK, BLOCK), BF16)
    tokens = jax.ShapeDtypeStruct((BLOCK, MODEL_WIDTH), BF16)
    grad = jax.ShapeDtypeStruct((SHARD, ADAPTER_RANK), F32)
    outs = pl.pallas_call(
        kernel,
        out_shape=(tokens, tokens, tokens, tokens, grad, grad),
        in_specs=[hbm, hbm, hbm, smem, hbm, vmem, vmem, vmem],
        out_specs=(vmem, hbm, hbm, hbm, vmem, vmem),
        scratch_shapes=[
            blocks3,
            blocks3,
            blocks3,
            blocks3,
            blocks3,
            blocks3,
            pltpu.VMEM((BLOCK, MODEL_WIDTH), BF16),
            blocks3,
            blocks3,
            blocks3,
            pltpu.VMEM((NZ, NX, 2, SHARD, MODEL_WIDTH), BF16),
            pltpu.VMEM((NZ, NX, 2, SHARD, 2 * ADAPTER_RANK), BF16),
            pltpu.VMEM((NB, KEY_BLOCKS * BLOCK, BLOCK), F32),
            pltpu.VMEM((NB, KEY_BLOCKS, BLOCK, BLOCK), BF16),
            pltpu.VMEM((NB, KEY_BLOCKS, BLOCK, BLOCK), BF16),
            pltpu.VMEM((RANDOM + 1, BLOCK, BLOCK), F32),
            pltpu.VMEM((RANDOM + 1, BLOCK, BLOCK), F32),
            pltpu.VMEM((BLOCK, 2 * ADAPTER_RANK), BF16),
            pltpu.VMEM((BLOCK, 2 * ADAPTER_RANK), BF16),
            pltpu.VMEM((NZ, NX, 2, SHARD, BLOCK), F32),
            pltpu.VMEM((NZ, NX, SHARD, BLOCK), F32),
            pltpu.VMEM((NZ, NX, SHARD, BLOCK), F32),
            pltpu.VMEM((NX, NZ, SHARD, BLOCK), F32),
            pltpu.VMEM((NZ, SHARD, BLOCK), F32),
            pltpu.VMEM((NZ, SHARD, BLOCK), F32),
            pltpu.VMEM((SHARD, BLOCK), F32),
            pltpu.VMEM((SHARD, BLOCK), F32),
            pltpu.VMEM((NY, 8, BLOCK), F32),
            pltpu.VMEM((NY, 8, BLOCK), F32),
            pltpu.VMEM((8, BLOCK), F32),
            pltpu.VMEM((NY, 8, BLOCK), F32),
            pltpu.SMEM((RANDOM,), jnp.int32),
            pltpu.SMEM((RANDOM,), jnp.int32),
            pltpu.SMEM((RANDOM,), F32),
            pltpu.SMEM((NB,), jnp.int32),
            pltpu.SMEM((NB,), F32),
            dma((3,)),
            dma((3,)),
            dma((5,)),
            dma((5,)),
            dma((3,)),
            dma((3,)),
            dma,
            dma((NZ,)),
            dma,
            dma((NZ, NX)),
            dma,
            dma((NZ, NX)),
            dma,
            dma((6,)),
            dma((6,)),
        ],
        compiler_params=pltpu.CompilerParams(
            collective_id=0, has_side_effects=True, vmem_limit_bytes=60 * 2**20
        ),
    )(q, k, v, jnp.transpose(blocks, (2, 0, 1)), w, a, b, cot)
    return pl.pallas_call(
        copy_out,
        out_shape=tuple(jax.ShapeDtypeStruct(o.shape, o.dtype) for o in outs),
        in_specs=[hbm] * len(outs),
        out_specs=(hbm,) * len(outs),
        scratch_shapes=[pltpu.VMEM(o.shape, o.dtype) for o in outs] + [dma((len(outs),)), dma((len(outs),))],
        compiler_params=pltpu.CompilerParams(vmem_limit_bytes=60 * 2**20),
    )(*outs)


def solution(mesh):
    rows = P(("fsdp", "sp"), None)
    return jax.shard_map(
        shards,
        mesh=mesh,
        in_specs=(rows, rows, rows, P("fsdp", None, None), P("fsdp", None), P("fsdp", None), P("fsdp", None), rows),
        out_specs=(rows, rows, rows, rows, P("fsdp", None), P("fsdp", None)),
        check_vma=False,
    )
```

```python
import math

import jax
import jax.numpy as jnp
from jax import lax
from jax.experimental import pallas as pl
from jax.experimental.pallas import tpu as pltpu
from jax.sharding import PartitionSpec as P

MODEL_WIDTH = 2048
HEADS = 16
BLOCK = 128
KEY_BLOCKS = 6
ADAPTER_RANK = 64
TOKENS = 65536

NZ, NX = 4, 4
NL, NY = 2, 8
NB = NL * NY
SHARD = 64
RANDOM = 2 * NB

MESH = pl.DeviceIdType.MESH
F32 = jnp.float32
BF16 = jnp.bfloat16


def dot(a, b, ca, cb):
    return lax.dot_general(a, b, (((ca,), (cb,)), ((), ())), preferred_element_type=F32)


def drain(ref, sem):
    pltpu.make_async_copy(ref, ref, sem).wait()


def kernel(
    q_ref,
    k_ref,
    v_ref,
    blk,
    w_ref,
    a_ref,
    b_ref,
    cot,
    mixed_ref,
    dq_ref,
    dk_ref,
    dv_ref,
    gd_ref,
    gu_ref,
    qh,
    kh,
    vh,
    gh,
    ctx_heads,
    dctx_send,
    ctx,
    dqb,
    dkb,
    dvb,
    wfull,
    ab,
    probs,
    wts,
    dsc,
    pre_k,
    pre_v,
    d0,
    l0,
    part,
    rc,
    s1,
    rx,
    s2,
    rz,
    s3,
    rl,
    s4,
    ry,
    s5,
    gfin,
    rank,
    perm,
    same,
    last,
    has,
    qkv_s,
    qkv_r,
    blk_s,
    blk_r,
    abz_s,
    abz_r,
    wz_s,
    wz_r,
    wx_s,
    wx_r,
    wc_s,
    wc_r,
    own_sem,
    red_s,
    red_r,
):
    f = lax.axis_index("fsdp")
    j = lax.axis_index("sp")
    z, x, c = f // (2 * NX), (f // 2) % NX, f % 2
    zl, y = j // NY, j % NY
    oc = 1 - c
    scaling = 1.0 / math.sqrt(BLOCK)
    log2e = 1.4426950408889634

    def fid(zz, xx, cc):
        return zz * (2 * NX) + xx * 2 + cc

    def sp_peer(d):
        return (j + d) % NB

    def peer(t):
        k = t // NL
        away = NY // 2 + (1 - 2 * (k % 2)) * ((k + 1) // 2)
        return ((zl + t % NL) % NL) * NY + (y + away) % NY

    sibling = (fid(z, x, oc), j)

    def xpeer(d):
        return (fid(z, (x + d) % NX, c), j)

    def zpeer(d):
        return (fid((z + d) % NZ, x, c), j)

    side = 1 - 2 * zl
    pair = (f, (1 - zl) * NY + y)
    outer = (fid((z - side + NZ) % NZ, x, c), (1 - zl) * NY + y)

    def remote(src, dst, ssem, rsem, dev):
        pltpu.make_async_remote_copy(
            src_ref=src, dst_ref=dst, send_sem=ssem, recv_sem=rsem, device_id=dev, device_id_type=MESH
        ).start()

    def cols(h):
        return pl.ds(pl.multiple_of(h * BLOCK, BLOCK), BLOCK)

    barrier = pltpu.get_barrier_semaphore()

    def greet(d, carry):
        pl.semaphore_signal(barrier, inc=1, device_id=(f, sp_peer(d)), device_id_type=MESH)
        return carry

    lax.fori_loop(1, NB, greet, 0)
    for d in (1, 2, 3):
        pl.semaphore_signal(barrier, inc=1, device_id=xpeer(d), device_id_type=MESH)
        pl.semaphore_signal(barrier, inc=1, device_id=zpeer(d), device_id_type=MESH)
    pl.semaphore_signal(barrier, inc=1, device_id=sibling, device_id_type=MESH)
    pl.semaphore_signal(barrier, inc=1, device_id=outer, device_id_type=MESH)
    pl.semaphore_wait(barrier, NB - 1 + 8)

    ab[z, x, c] = jnp.concatenate([a_ref[...], b_ref[...]], axis=1)
    for d in (1, 3, 2):
        remote(ab.at[z, x, c], ab.at[z, x, c], abz_s.at[0], abz_r.at[0], zpeer(d))

    for n, (src, dst) in enumerate(((k_ref, kh), (q_ref, qh), (v_ref, vh))):

        def send_heads(t, carry, src=src, dst=dst, n=n):
            h = peer(t + t // (NB - 2))
            remote(src.at[:, cols(h)], dst.at[j], qkv_s.at[n], qkv_r.at[n], (f, h))
            return carry

        lax.fori_loop(0, NB - 1, send_heads, 0)
        pltpu.make_async_copy(src.at[:, cols(j)], dst.at[j], qkv_r.at[n]).start()
        if n == 0:
            remote(w_ref, wfull.at[z, x, c], wz_s, wz_r.at[z], outer)
            pltpu.make_async_copy(w_ref, wfull.at[z, x, c], own_sem).start()
            remote(w_ref, wfull.at[z, x, c], wc_s, wc_r.at[z, x], sibling)
            drain(ab.at[0, pl.ds(0, 3), 0], abz_r.at[0])
            for d in (1, 3, 2):
                remote(ab.at[:, x, c], ab.at[:, x, c], abz_s.at[1], abz_r.at[1], xpeer(d))
            for d in (1, 3):
                remote(w_ref, wfull.at[z, x, c], wx_s, wx_r.at[z, x], xpeer(d))

    def entry(r):
        return blk[4 + r % 2, 0, r // 2]

    def rank_of(r, carry):
        mine = entry(r) * RANDOM + r
        total = jnp.int32(0)
        for s in range(RANDOM):
            total = total + jnp.where(entry(s) * RANDOM + s < mine, 1, 0)
        rank[r] = total
        return carry

    lax.fori_loop(0, RANDOM, rank_of, 0)

    def perm_of(p, carry):
        total = jnp.int32(0)
        for s in range(RANDOM):
            total = total + jnp.where(rank[s] == p, s, 0)
        perm[p] = total
        named = blk[4 + total % 2, 0, total // 2]
        same[p] = jnp.where(named == carry, 1.0, 0.0).astype(F32)
        return named

    lax.fori_loop(0, RANDOM, perm_of, jnp.int32(-1))

    def last_of(n, carry):
        upto = jnp.int32(0)
        equal = jnp.int32(0)
        for s in range(RANDOM):
            upto = upto + jnp.where(entry(s) <= n, 1, 0)
            equal = equal + jnp.where(entry(s) == n, 1, 0)
        last[n] = jnp.maximum(upto - 1, 0)
        has[n] = jnp.where(equal > 0, 1.0, 0.0).astype(F32)
        return carry

    lax.fori_loop(0, NB, last_of, 0)

    drain(ab.at[pl.ds(0, 3), :, 0], abz_r.at[1])
    remote(ab.at[:, :, c], ab.at[:, :, c], abz_s.at[2], abz_r.at[2], sibling)

    mine, near, next_, far = z, (z - side + NZ) % NZ, (z + side + NZ) % NZ, (z + 2) % NZ
    left, right = (x + NX - 1) % NX, (x + 1) % NX
    half = SHARD // 2

    def forward_z(u, onward):
        piece = wfull.at[u, x, c]
        drain(piece, wz_r.at[u])
        if onward is not None:
            remote(piece, piece, wz_s, wz_r.at[u], onward)
        for e in (1, 3):
            remote(piece, piece, wx_s, wx_r.at[u, x], xpeer(e))
        remote(piece, piece, wc_s, wc_r.at[u, x], sibling)

    def forward_x(u):
        for xx, start, e in ((left, 0, 1), (right, half, 3)):
            piece = wfull.at[u, xx, c]
            drain(piece, wx_r.at[u, xx])
            part_ = wfull.at[u, xx, c, pl.ds(start, half)]
            remote(part_, part_, wx_s, wx_r.at[u, xx], xpeer(e))
            remote(piece, piece, wc_s, wc_r.at[u, xx], sibling)

    def forward_last(u):
        xx = (x + 2) % NX
        piece = wfull.at[u, xx, c]
        drain(piece, wx_r.at[u, xx])
        remote(piece, piece, wc_s, wc_r.at[u, xx], sibling)

    def context_gradient(u):
        def one_head(e, carry):
            xx = (x + e) % NX
            h = u * NX + xx
            drain(wfull.at[u, xx, oc], wc_r.at[u, xx])
            rows = wfull[u, xx].reshape(BLOCK, MODEL_WIDTH)
            adapter = ab[u, xx].reshape(BLOCK, 2 * ADAPTER_RANK)
            g = dot(cot[...], rows, 1, 1) + dot(d0[...], adapter, 1, 1)
            dctx_send[h] = g.astype(BF16)

            @pl.when(h != j)
            def _():
                remote(dctx_send.at[h], gh.at[j], blk_s.at[1], blk_r.at[1], (f, h))

            @pl.when(h == j)
            def _():
                pltpu.make_async_copy(dctx_send.at[h], gh.at[j], blk_r.at[1]).start()

            return carry

        lax.fori_loop(0, NX, one_head, 0)

    forward_z(near, pair)
    forward_x(mine)
    forward_z(next_, outer)
    forward_last(mine)

    drain(w_ref, own_sem)
    drain(ab.at[:, :, 0], abz_r.at[2])
    lane = lax.broadcasted_iota(jnp.int32, (BLOCK, 2 * ADAPTER_RANK), 1)
    both = dot(cot[...], ab[...].reshape(MODEL_WIDTH, 2 * ADAPTER_RANK), 1, 0)
    d0[...] = jnp.where(lane < ADAPTER_RANK, pltpu.roll(both, ADAPTER_RANK, 1), 0.0).astype(BF16)

    context_gradient(mine)
    forward_x(near)
    forward_z(far, None)
    forward_last(near)
    context_gradient(near)
    forward_x(next_)
    forward_last(next_)
    context_gradient(next_)
    forward_x(far)

    drain(kh, qkv_r.at[0])
    drain(qh, qkv_r.at[1])
    drain(vh, qkv_r.at[2])

    def gathered(ref, i):
        return jnp.concatenate([ref[blk[s, 0, i]] for s in range(KEY_BLOCKS)], axis=0)

    def send_block(src, dst_ref, n, i):
        @pl.when(i != j)
        def _():
            remote(src.at[i], dst_ref.at[:, cols(j)], blk_s.at[n], blk_r.at[n], (f, i))

        @pl.when(i == j)
        def _():
            pltpu.make_async_copy(src.at[i], dst_ref.at[:, cols(j)], blk_r.at[n]).start()

    def forward_block(t, carry):
        i = peer(t)
        scores = dot(gathered(kh, i), qh[i], 1, 1)
        highest = jnp.max(scores, axis=0, keepdims=True)
        raised = jnp.exp2((scores - highest) * (scaling * log2e))
        p = raised * (1.0 / jnp.sum(raised, axis=0, keepdims=True))
        probs[i] = p
        w = p.astype(BF16)
        wts[i] = w.reshape(KEY_BLOCKS, BLOCK, BLOCK)
        ctx_heads[i] = dot(w, gathered(vh, i), 0, 0).astype(BF16)
        send_block(ctx_heads, ctx, 0, i)
        return carry

    lax.fori_loop(0, NB, forward_block, 0, unroll=2)

    forward_last(far)

    context_gradient(far)

    drain(ctx, blk_r.at[0])
    both = dot(ctx[...], ab[...].reshape(MODEL_WIDTH, 2 * ADAPTER_RANK), 1, 0)
    low = jnp.where(lane >= ADAPTER_RANK, pltpu.roll(both, ADAPTER_RANK, 1), 0.0).astype(BF16)
    l0[...] = low
    normal = 1.0 / math.sqrt(TOKENS)

    def partial(h, carry):
        s = dot(ctx[:, cols(h)], d0[...], 0, 0) + dot(cot[:, cols(h)], l0[...], 0, 0)
        part[h // NX, h % NX] = (s * normal).reshape(2, SHARD, BLOCK)
        return carry

    lax.fori_loop(0, HEADS, partial, 0, unroll=2)
    remote(part.at[:, :, oc], rc, red_s.at[0], red_r.at[0], sibling)

    drain(gh, blk_r.at[1])

    def backward_block(t, carry):
        i = peer(t)
        p = probs[i]
        dw = dot(gathered(vh, i), gh[i], 1, 1)
        correction = jnp.sum(p * dw, axis=0, keepdims=True)
        ds = (p * (dw - correction) * scaling).astype(BF16)
        dsc[i] = ds.reshape(KEY_BLOCKS, BLOCK, BLOCK)
        dqb[i] = dot(ds, gathered(kh, i), 0, 0).astype(BF16)
        send_block(dqb, dq_ref, 2, i)
        return carry

    lax.fori_loop(0, NB, backward_block, 0, unroll=2)

    drain(rc, red_r.at[0])

    def add_core(u, carry):
        s1[u] = part[u, :, c] + rc[u]
        return carry

    lax.fori_loop(0, NZ, add_core, 0)
    for e in (1, 3, 2):
        remote(s1.at[:, (x + e) % NX], rx.at[x], red_s.at[1], red_r.at[1], xpeer(e))

    def random_terms(p, carry):
        r = perm[p]
        i = r // 2
        slot = 4 + r % 2
        keep = same[p]
        acc_k = carry[0] * keep + dot(dsc[i, slot], qh[i], 1, 0)
        acc_v = carry[1] * keep + dot(wts[i, slot], gh[i], 1, 0)
        pre_k[p] = acc_k
        pre_v[p] = acc_v
        return acc_k, acc_v

    zero = jnp.zeros((BLOCK, BLOCK), F32)
    lax.fori_loop(0, RANDOM, random_terms, (zero, zero), unroll=4)

    def long_dot(terms, rows):
        wide = jnp.concatenate(terms, axis=1)
        return dot(wide, jnp.concatenate(rows, axis=0), 1, 0)

    every = range(NB)
    pre_k[RANDOM] = long_dot([dsc[i, 3] for i in every], [qh[i] for i in every])
    pre_v[RANDOM] = long_dot([wts[i, 3] for i in every], [gh[i] for i in every])
    common = blk[3, 0, 0]

    def key_block(t, carry):
        n = peer(t)
        before, after = (n + NB - 1) % NB, (n + 1) % NB
        slot_before = jnp.where(blk[2, 0, before] == n, 2, 0)
        slot_after = jnp.where(blk[0, 0, after] == n, 0, 2)
        is_common = jnp.where(common == n, 1.0, 0.0).astype(F32)

        def total(terms, rows, pre):
            window = long_dot(
                [terms[n, 1], terms[before, slot_before], terms[after, slot_after]],
                [rows[n], rows[before], rows[after]],
            )
            return (window + pre[last[n]] * has[n] + pre[RANDOM] * is_common).astype(BF16)

        dkb[n] = total(dsc, qh, pre_k)
        send_block(dkb, dk_ref, 3, n)
        dvb[n] = total(wts, gh, pre_v)
        send_block(dvb, dv_ref, 4, n)
        return carry

    lax.fori_loop(0, NB, key_block, 0)

    drain(rx.at[pl.ds(0, 3)], red_r.at[1])
    s2[...] = s1[:, x] + rx[(x + 1) % NX] + rx[(x + 2) % NX] + rx[(x + 3) % NX]
    for e in (1, 3, 2):
        remote(s2.at[(z + e) % NZ], rz.at[z], red_s.at[2], red_r.at[2], zpeer(e))

    wide = 256

    def output_columns(n, carry):
        rows = wfull[:, :, :, :, pl.ds(pl.multiple_of(n * wide, wide), wide)]
        adapter = ab[n // 2, pl.ds(2 * (n % 2), 2)].reshape(wide, 2 * ADAPTER_RANK)
        m = dot(ctx[...], rows.reshape(MODEL_WIDTH, wide), 1, 0) + dot(l0[...], adapter, 1, 1)
        mixed_ref[:, pl.ds(pl.multiple_of(n * wide, wide), wide)] = m.astype(BF16)
        return carry

    lax.fori_loop(0, MODEL_WIDTH // wide, output_columns, 0)

    drain(rz.at[pl.ds(0, 3)], red_r.at[2])
    s3[...] = s2[z] + rz[(z + 1) % NZ] + rz[(z + 2) % NZ] + rz[(z + 3) % NZ]
    remote(s3, rl, red_s.at[3], red_r.at[3], (f, (1 - zl) * NY + y))
    drain(rl, red_r.at[3])
    s4[...] = (s3[...] + rl[...]).reshape(NY, 8, BLOCK)
    for e in range(1, NY):
        yy = (y + e) % NY
        remote(s4.at[yy], ry.at[y], red_s.at[4], red_r.at[4], (f, zl * NY + yy))
    drain(ry.at[pl.ds(0, NY - 1)], red_r.at[4])
    total = s4[y]
    for e in range(1, NY):
        total = total + ry[(y + e) % NY]
    s5[...] = total
    gfin[y] = total
    for e in range(1, NY):
        yy = (y + e) % NY
        remote(s5, gfin.at[y], red_s.at[5], red_r.at[5], (f, zl * NY + yy))
    drain(ry.at[pl.ds(0, NY - 1)], red_r.at[5])
    both = gfin[...].reshape(SHARD, BLOCK)
    gd_ref[...] = both[:, :ADAPTER_RANK]
    gu_ref[...] = both[:, ADAPTER_RANK:]

    drain(dq_ref, blk_r.at[2])
    drain(dk_ref, blk_r.at[3])
    drain(dv_ref, blk_r.at[4])
    for n in range(3):
        drain(qh.at[pl.ds(0, NB - 1)], qkv_s.at[n])
    for n in range(5):
        drain(qh.at[pl.ds(0, NB - 1)], blk_s.at[n])
    drain(ab.at[0, pl.ds(0, 3), 0], abz_s.at[0])
    drain(ab.at[pl.ds(0, 3), :, 0], abz_s.at[1])
    drain(ab.at[:, :, 0], abz_s.at[2])
    drain(wfull.at[0, pl.ds(0, 3), 0], wz_s)
    drain(wfull.at[pl.ds(0, 3), :, 0], wx_s)
    drain(wfull.at[:, :, 0], wc_s)
    drain(rc, red_s.at[0])
    drain(rx.at[pl.ds(0, 3)], red_s.at[1])
    drain(rz.at[pl.ds(0, 3)], red_s.at[2])
    drain(rl, red_s.at[3])
    drain(ry.at[pl.ds(0, NY - 1)], red_s.at[4])
    drain(ry.at[pl.ds(0, NY - 1)], red_s.at[5])


def copy_out(*refs):
    n = (len(refs) - 2) // 3
    sources, targets, held = refs[:n], refs[n : 2 * n], refs[2 * n : 3 * n]
    in_sem, out_sem = refs[3 * n :]
    inward = [pltpu.make_async_copy(sources[i], held[i], in_sem.at[i]) for i in range(n)]
    outward = [pltpu.make_async_copy(held[i], targets[i], out_sem.at[i]) for i in range(n)]
    for copy in inward:
        copy.start()
    for i in range(n):
        inward[i].wait()
        outward[i].start()
    for copy in outward:
        copy.wait()


def shards(q, k, v, blocks, w, a, b, cot):
    hbm = pl.BlockSpec(memory_space=pl.ANY)
    vmem = pl.BlockSpec(memory_space=pltpu.VMEM)
    smem = pl.BlockSpec(memory_space=pltpu.SMEM)
    dma = pltpu.SemaphoreType.DMA
    blocks3 = pltpu.VMEM((NB, BLOCK, BLOCK), BF16)
    tokens = jax.ShapeDtypeStruct((BLOCK, MODEL_WIDTH), BF16)
    grad = jax.ShapeDtypeStruct((SHARD, ADAPTER_RANK), F32)
    outs = pl.pallas_call(
        kernel,
        out_shape=(tokens, tokens, tokens, tokens, grad, grad),
        in_specs=[hbm, hbm, hbm, smem, hbm, vmem, vmem, vmem],
        out_specs=(vmem, hbm, hbm, hbm, vmem, vmem),
        scratch_shapes=[
            blocks3,
            blocks3,
            blocks3,
            blocks3,
            blocks3,
            blocks3,
            pltpu.VMEM((BLOCK, MODEL_WIDTH), BF16),
            blocks3,
            blocks3,
            blocks3,
            pltpu.VMEM((NZ, NX, 2, SHARD, MODEL_WIDTH), BF16),
            pltpu.VMEM((NZ, NX, 2, SHARD, 2 * ADAPTER_RANK), BF16),
            pltpu.VMEM((NB, KEY_BLOCKS * BLOCK, BLOCK), F32),
            pltpu.VMEM((NB, KEY_BLOCKS, BLOCK, BLOCK), BF16),
            pltpu.VMEM((NB, KEY_BLOCKS, BLOCK, BLOCK), BF16),
            pltpu.VMEM((RANDOM + 1, BLOCK, BLOCK), F32),
            pltpu.VMEM((RANDOM + 1, BLOCK, BLOCK), F32),
            pltpu.VMEM((BLOCK, 2 * ADAPTER_RANK), BF16),
            pltpu.VMEM((BLOCK, 2 * ADAPTER_RANK), BF16),
            pltpu.VMEM((NZ, NX, 2, SHARD, BLOCK), F32),
            pltpu.VMEM((NZ, NX, SHARD, BLOCK), F32),
            pltpu.VMEM((NZ, NX, SHARD, BLOCK), F32),
            pltpu.VMEM((NX, NZ, SHARD, BLOCK), F32),
            pltpu.VMEM((NZ, SHARD, BLOCK), F32),
            pltpu.VMEM((NZ, SHARD, BLOCK), F32),
            pltpu.VMEM((SHARD, BLOCK), F32),
            pltpu.VMEM((SHARD, BLOCK), F32),
            pltpu.VMEM((NY, 8, BLOCK), F32),
            pltpu.VMEM((NY, 8, BLOCK), F32),
            pltpu.VMEM((8, BLOCK), F32),
            pltpu.VMEM((NY, 8, BLOCK), F32),
            pltpu.SMEM((RANDOM,), jnp.int32),
            pltpu.SMEM((RANDOM,), jnp.int32),
            pltpu.SMEM((RANDOM,), F32),
            pltpu.SMEM((NB,), jnp.int32),
            pltpu.SMEM((NB,), F32),
            dma((3,)),
            dma((3,)),
            dma((5,)),
            dma((5,)),
            dma((3,)),
            dma((3,)),
            dma,
            dma((NZ,)),
            dma,
            dma((NZ, NX)),
            dma,
            dma((NZ, NX)),
            dma,
            dma((6,)),
            dma((6,)),
        ],
        compiler_params=pltpu.CompilerParams(
            collective_id=0, has_side_effects=True, vmem_limit_bytes=60 * 2**20
        ),
    )(q, k, v, jnp.transpose(blocks, (2, 0, 1)), w, a, b, cot)
    return pl.pallas_call(
        copy_out,
        out_shape=tuple(jax.ShapeDtypeStruct(o.shape, o.dtype) for o in outs),
        in_specs=[hbm] * len(outs),
        out_specs=(hbm,) * len(outs),
        scratch_shapes=[pltpu.VMEM(o.shape, o.dtype) for o in outs] + [dma((len(outs),)), dma((len(outs),))],
        compiler_params=pltpu.CompilerParams(vmem_limit_bytes=60 * 2**20),
    )(*outs)


def solution(mesh):
    rows = P(("fsdp", "sp"), None)
    return jax.shard_map(
        shards,
        mesh=mesh,
        in_specs=(rows, rows, rows, P("fsdp", None, None), P("fsdp", None), P("fsdp", None), P("fsdp", None), rows),
        out_specs=(rows, rows, rows, rows, P("fsdp", None), P("fsdp", None)),
        check_vma=False,
    )
```

```python
import math

import jax
import jax.numpy as jnp
from jax import lax
from jax.experimental import pallas as pl
from jax.experimental.pallas import tpu as pltpu
from jax.sharding import PartitionSpec as P

MODEL_WIDTH = 2048
HEADS = 16
BLOCK = 128
KEY_BLOCKS = 6
ADAPTER_RANK = 64
TOKENS = 65536

NZ, NX = 4, 4
NL, NY = 2, 8
NB = NL * NY
SHARD = 64
RANDOM = 2 * NB

MESH = pl.DeviceIdType.MESH
F32 = jnp.float32
BF16 = jnp.bfloat16


def dot(a, b, ca, cb):
    return lax.dot_general(a, b, (((ca,), (cb,)), ((), ())), preferred_element_type=F32)


def drain(ref, sem):
    pltpu.make_async_copy(ref, ref, sem).wait()


def kernel(
    q_ref,
    k_ref,
    v_ref,
    blk,
    w_ref,
    a_ref,
    b_ref,
    cot,
    mixed_ref,
    dq_ref,
    dk_ref,
    dv_ref,
    gd_ref,
    gu_ref,
    qh,
    kh,
    vh,
    gh,
    ctx_heads,
    dctx_send,
    ctx,
    dqb,
    dkb,
    dvb,
    wfull,
    ab,
    probs,
    wts,
    dsc,
    pre_k,
    pre_v,
    d0,
    l0,
    part,
    rc,
    s1,
    rx,
    s2,
    rz,
    s3,
    rl,
    s4,
    ry,
    s5,
    gfin,
    rank,
    perm,
    same,
    last,
    has,
    qkv_s,
    qkv_r,
    blk_s,
    blk_r,
    abz_s,
    abz_r,
    wz_s,
    wz_r,
    wx_s,
    wx_r,
    wc_s,
    wc_r,
    own_sem,
    gh_r,
    red_s,
    red_r,
):
    f = lax.axis_index("fsdp")
    j = lax.axis_index("sp")
    z, x, c = f // (2 * NX), (f // 2) % NX, f % 2
    zl, y = j // NY, j % NY
    oc = 1 - c
    scaling = 1.0 / math.sqrt(BLOCK)
    log2e = 1.4426950408889634

    def fid(zz, xx, cc):
        return zz * (2 * NX) + xx * 2 + cc

    def sp_peer(d):
        return (j + d) % NB

    def peer(t):
        k = t // NL
        away = NY // 2 + (1 - 2 * (k % 2)) * ((k + 1) // 2)
        return ((zl + t % NL) % NL) * NY + (y + away) % NY

    sibling = (fid(z, x, oc), j)

    def xpeer(d):
        return (fid(z, (x + d) % NX, c), j)

    def zpeer(d):
        return (fid((z + d) % NZ, x, c), j)

    side = 1 - 2 * zl
    pair = (f, (1 - zl) * NY + y)
    outer = (fid((z - side + NZ) % NZ, x, c), (1 - zl) * NY + y)

    def remote(src, dst, ssem, rsem, dev):
        pltpu.make_async_remote_copy(
            src_ref=src, dst_ref=dst, send_sem=ssem, recv_sem=rsem, device_id=dev, device_id_type=MESH
        ).start()

    def cols(h):
        return pl.ds(pl.multiple_of(h * BLOCK, BLOCK), BLOCK)

    barrier = pltpu.get_barrier_semaphore()

    def greet(d, carry):
        pl.semaphore_signal(barrier, inc=1, device_id=(f, sp_peer(d)), device_id_type=MESH)
        return carry

    lax.fori_loop(1, NB, greet, 0)
    for d in (1, 2, 3):
        pl.semaphore_signal(barrier, inc=1, device_id=xpeer(d), device_id_type=MESH)
        pl.semaphore_signal(barrier, inc=1, device_id=zpeer(d), device_id_type=MESH)
    pl.semaphore_signal(barrier, inc=1, device_id=sibling, device_id_type=MESH)
    pl.semaphore_signal(barrier, inc=1, device_id=outer, device_id_type=MESH)
    pl.semaphore_wait(barrier, NB - 1 + 8)

    ab[z, x, c] = jnp.concatenate([a_ref[...], b_ref[...]], axis=1)
    for d in (1, 3, 2):
        remote(ab.at[z, x, c], ab.at[z, x, c], abz_s.at[0], abz_r.at[0], zpeer(d))

    for n, (src, dst) in enumerate(((k_ref, kh), (q_ref, qh), (v_ref, vh))):

        def send_heads(t, carry, src=src, dst=dst, n=n):
            h = peer(t + t // (NB - 2))
            remote(src.at[:, cols(h)], dst.at[j], qkv_s.at[n], qkv_r.at[n], (f, h))
            return carry

        lax.fori_loop(0, NB - 1, send_heads, 0)
        pltpu.make_async_copy(src.at[:, cols(j)], dst.at[j], qkv_r.at[n]).start()
        if n == 0:
            remote(w_ref, wfull.at[z, x, c], wz_s, wz_r.at[z], outer)
            pltpu.make_async_copy(w_ref, wfull.at[z, x, c], own_sem).start()
            remote(w_ref, wfull.at[z, x, c], wc_s, wc_r.at[z, x], sibling)
            drain(ab.at[0, pl.ds(0, 3), 0], abz_r.at[0])
            for d in (1, 3, 2):
                remote(ab.at[:, x, c], ab.at[:, x, c], abz_s.at[1], abz_r.at[1], xpeer(d))
            for d in (1, 3):
                remote(w_ref, wfull.at[z, x, c], wx_s, wx_r.at[z, x], xpeer(d))

    def entry(r):
        return blk[4 + r % 2, 0, r // 2]

    def rank_of(r, carry):
        mine = entry(r) * RANDOM + r
        total = jnp.int32(0)
        for s in range(RANDOM):
            total = total + jnp.where(entry(s) * RANDOM + s < mine, 1, 0)
        rank[r] = total
        return carry

    lax.fori_loop(0, RANDOM, rank_of, 0)

    def perm_of(p, carry):
        total = jnp.int32(0)
        for s in range(RANDOM):
            total = total + jnp.where(rank[s] == p, s, 0)
        perm[p] = total
        named = blk[4 + total % 2, 0, total // 2]
        same[p] = jnp.where(named == carry, 1.0, 0.0).astype(F32)
        return named

    lax.fori_loop(0, RANDOM, perm_of, jnp.int32(-1))

    def last_of(n, carry):
        upto = jnp.int32(0)
        equal = jnp.int32(0)
        for s in range(RANDOM):
            upto = upto + jnp.where(entry(s) <= n, 1, 0)
            equal = equal + jnp.where(entry(s) == n, 1, 0)
        last[n] = jnp.maximum(upto - 1, 0)
        has[n] = jnp.where(equal > 0, 1.0, 0.0).astype(F32)
        return carry

    lax.fori_loop(0, NB, last_of, 0)

    drain(ab.at[pl.ds(0, 3), :, 0], abz_r.at[1])
    remote(ab.at[:, :, c], ab.at[:, :, c], abz_s.at[2], abz_r.at[2], sibling)

    mine, near, next_, far = z, (z - side + NZ) % NZ, (z + side + NZ) % NZ, (z + 2) % NZ
    left, right = (x + NX - 1) % NX, (x + 1) % NX
    half = SHARD // 2

    def forward_z(u, onward):
        piece = wfull.at[u, x, c]
        drain(piece, wz_r.at[u])
        if onward is not None:
            remote(piece, piece, wz_s, wz_r.at[u], onward)
        for e in (1, 3):
            remote(piece, piece, wx_s, wx_r.at[u, x], xpeer(e))
        remote(piece, piece, wc_s, wc_r.at[u, x], sibling)

    def forward_x(u):
        for xx, start, e in ((left, 0, 1), (right, half, 3)):
            piece = wfull.at[u, xx, c]
            drain(piece, wx_r.at[u, xx])
            part_ = wfull.at[u, xx, c, pl.ds(start, half)]
            remote(part_, part_, wx_s, wx_r.at[u, xx], xpeer(e))
            remote(piece, piece, wc_s, wc_r.at[u, xx], sibling)

    def forward_last(u):
        xx = (x + 2) % NX
        piece = wfull.at[u, xx, c]
        drain(piece, wx_r.at[u, xx])
        remote(piece, piece, wc_s, wc_r.at[u, xx], sibling)

    forward_z(near, pair)
    forward_x(mine)
    forward_z(next_, outer)
    forward_last(mine)

    drain(w_ref, own_sem)
    drain(ab.at[:, :, 0], abz_r.at[2])
    lane = lax.broadcasted_iota(jnp.int32, (BLOCK, 2 * ADAPTER_RANK), 1)
    both = dot(cot[...], ab[...].reshape(MODEL_WIDTH, 2 * ADAPTER_RANK), 1, 0)
    d0[...] = jnp.where(lane < ADAPTER_RANK, pltpu.roll(both, ADAPTER_RANK, 1), 0.0).astype(BF16)

    forward_x(near)
    forward_z(far, None)
    forward_last(near)
    forward_x(next_)
    forward_last(next_)
    forward_x(far)

    drain(kh, qkv_r.at[0])
    drain(qh, qkv_r.at[1])
    drain(vh, qkv_r.at[2])

    def gathered(ref, i):
        return jnp.concatenate([ref[blk[s, 0, i]] for s in range(KEY_BLOCKS)], axis=0)

    def send_block(src, dst_ref, n, i):
        @pl.when(i != j)
        def _():
            remote(src.at[i], dst_ref.at[:, cols(j)], blk_s.at[n], blk_r.at[n], (f, i))

        @pl.when(i == j)
        def _():
            pltpu.make_async_copy(src.at[i], dst_ref.at[:, cols(j)], blk_r.at[n]).start()

    def forward_block(t, carry):
        i = peer(t)
        scores = dot(gathered(kh, i), qh[i], 1, 1)
        highest = jnp.max(scores, axis=0, keepdims=True)
        raised = jnp.exp2((scores - highest) * (scaling * log2e))
        p = raised * (1.0 / jnp.sum(raised, axis=0, keepdims=True))
        probs[i] = p
        w = p.astype(BF16)
        wts[i] = w.reshape(KEY_BLOCKS, BLOCK, BLOCK)
        ctx_heads[i] = dot(w, gathered(vh, i), 0, 0).astype(BF16)
        send_block(ctx_heads, ctx, 0, i)
        return carry

    lax.fori_loop(0, NB, forward_block, 0, unroll=2)

    forward_last(far)

    def context_gradient(t, carry):
        h = peer(t)
        u, xx = h // NX, h % NX
        drain(wfull.at[u, xx, oc], wc_r.at[u, xx])
        rows = wfull[u, xx].reshape(BLOCK, MODEL_WIDTH)
        adapter = ab[u, xx].reshape(BLOCK, 2 * ADAPTER_RANK)
        g = dot(cot[...], rows, 1, 1) + dot(d0[...], adapter, 1, 1)
        dctx_send[h] = g.astype(BF16)

        @pl.when(h != j)
        def _():
            remote(dctx_send.at[h], gh.at[j], blk_s.at[1], gh_r.at[j], (f, h))

        @pl.when(h == j)
        def _():
            pltpu.make_async_copy(dctx_send.at[h], gh.at[j], gh_r.at[j]).start()

        return carry

    lax.fori_loop(0, NB, context_gradient, 0, unroll=2)

    drain(ctx, blk_r.at[0])
    both = dot(ctx[...], ab[...].reshape(MODEL_WIDTH, 2 * ADAPTER_RANK), 1, 0)
    low = jnp.where(lane >= ADAPTER_RANK, pltpu.roll(both, ADAPTER_RANK, 1), 0.0).astype(BF16)
    l0[...] = low
    normal = 1.0 / math.sqrt(TOKENS)

    def partial(h, carry):
        s = dot(ctx[:, cols(h)], d0[...], 0, 0) + dot(cot[:, cols(h)], l0[...], 0, 0)
        part[h // NX, h % NX] = (s * normal).reshape(2, SHARD, BLOCK)
        return carry

    lax.fori_loop(0, HEADS, partial, 0, unroll=2)
    remote(part.at[:, :, oc], rc, red_s.at[0], red_r.at[0], sibling)

    def backward_block(t, carry):
        i = peer(t)
        drain(gh.at[i], gh_r.at[i])
        p = probs[i]
        dw = dot(gathered(vh, i), gh[i], 1, 1)
        correction = jnp.sum(p * dw, axis=0, keepdims=True)
        ds = (p * (dw - correction) * scaling).astype(BF16)
        dsc[i] = ds.reshape(KEY_BLOCKS, BLOCK, BLOCK)
        dqb[i] = dot(ds, gathered(kh, i), 0, 0).astype(BF16)
        send_block(dqb, dq_ref, 2, i)
        return carry

    lax.fori_loop(0, NB, backward_block, 0, unroll=2)

    drain(rc, red_r.at[0])

    def add_core(u, carry):
        s1[u] = part[u, :, c] + rc[u]
        return carry

    lax.fori_loop(0, NZ, add_core, 0)
    for e in (1, 3, 2):
        remote(s1.at[:, (x + e) % NX], rx.at[x], red_s.at[1], red_r.at[1], xpeer(e))

    def random_terms(p, carry):
        r = perm[p]
        i = r // 2
        slot = 4 + r % 2
        keep = same[p]
        acc_k = carry[0] * keep + dot(dsc[i, slot], qh[i], 1, 0)
        acc_v = carry[1] * keep + dot(wts[i, slot], gh[i], 1, 0)
        pre_k[p] = acc_k
        pre_v[p] = acc_v
        return acc_k, acc_v

    zero = jnp.zeros((BLOCK, BLOCK), F32)
    lax.fori_loop(0, RANDOM, random_terms, (zero, zero), unroll=8)

    def long_dot(terms, rows):
        wide = jnp.concatenate(terms, axis=1)
        return dot(wide, jnp.concatenate(rows, axis=0), 1, 0)

    every = range(NB)
    pre_k[RANDOM] = long_dot([dsc[i, 3] for i in every], [qh[i] for i in every])
    pre_v[RANDOM] = long_dot([wts[i, 3] for i in every], [gh[i] for i in every])
    common = blk[3, 0, 0]

    def key_block(t, carry):
        n = peer(t)
        before, after = (n + NB - 1) % NB, (n + 1) % NB
        slot_before = jnp.where(blk[2, 0, before] == n, 2, 0)
        slot_after = jnp.where(blk[0, 0, after] == n, 0, 2)
        is_common = jnp.where(common == n, 1.0, 0.0).astype(F32)

        def total(terms, rows, pre):
            window = long_dot(
                [terms[n, 1], terms[before, slot_before], terms[after, slot_after]],
                [rows[n], rows[before], rows[after]],
            )
            return (window + pre[last[n]] * has[n] + pre[RANDOM] * is_common).astype(BF16)

        dkb[n] = total(dsc, qh, pre_k)
        send_block(dkb, dk_ref, 3, n)
        dvb[n] = total(wts, gh, pre_v)
        send_block(dvb, dv_ref, 4, n)
        return carry

    lax.fori_loop(0, NB, key_block, 0)

    drain(rx.at[pl.ds(0, 3)], red_r.at[1])
    s2[...] = s1[:, x] + rx[(x + 1) % NX] + rx[(x + 2) % NX] + rx[(x + 3) % NX]
    for e in (1, 3, 2):
        remote(s2.at[(z + e) % NZ], rz.at[z], red_s.at[2], red_r.at[2], zpeer(e))

    wide = 256

    def output_columns(n, carry):
        rows = wfull[:, :, :, :, pl.ds(pl.multiple_of(n * wide, wide), wide)]
        adapter = ab[n // 2, pl.ds(2 * (n % 2), 2)].reshape(wide, 2 * ADAPTER_RANK)
        m = dot(ctx[...], rows.reshape(MODEL_WIDTH, wide), 1, 0) + dot(l0[...], adapter, 1, 1)
        mixed_ref[:, pl.ds(pl.multiple_of(n * wide, wide), wide)] = m.astype(BF16)
        return carry

    lax.fori_loop(0, MODEL_WIDTH // wide, output_columns, 0)

    drain(rz.at[pl.ds(0, 3)], red_r.at[2])
    s3[...] = s2[z] + rz[(z + 1) % NZ] + rz[(z + 2) % NZ] + rz[(z + 3) % NZ]
    remote(s3, rl, red_s.at[3], red_r.at[3], (f, (1 - zl) * NY + y))
    drain(rl, red_r.at[3])
    s4[...] = (s3[...] + rl[...]).reshape(NY, 8, BLOCK)
    for e in range(1, NY):
        yy = (y + e) % NY
        remote(s4.at[yy], ry.at[y], red_s.at[4], red_r.at[4], (f, zl * NY + yy))
    drain(ry.at[pl.ds(0, NY - 1)], red_r.at[4])
    total = s4[y]
    for e in range(1, NY):
        total = total + ry[(y + e) % NY]
    s5[...] = total
    gfin[y] = total
    for e in range(1, NY):
        yy = (y + e) % NY
        remote(s5, gfin.at[y], red_s.at[5], red_r.at[5], (f, zl * NY + yy))
    drain(ry.at[pl.ds(0, NY - 1)], red_r.at[5])
    both = gfin[...].reshape(SHARD, BLOCK)
    gd_ref[...] = both[:, :ADAPTER_RANK]
    gu_ref[...] = both[:, ADAPTER_RANK:]

    drain(dq_ref, blk_r.at[2])
    drain(dk_ref, blk_r.at[3])
    drain(dv_ref, blk_r.at[4])
    for n in range(3):
        drain(qh.at[pl.ds(0, NB - 1)], qkv_s.at[n])
    for n in range(5):
        drain(qh.at[pl.ds(0, NB - 1)], blk_s.at[n])
    drain(ab.at[0, pl.ds(0, 3), 0], abz_s.at[0])
    drain(ab.at[pl.ds(0, 3), :, 0], abz_s.at[1])
    drain(ab.at[:, :, 0], abz_s.at[2])
    drain(wfull.at[0, pl.ds(0, 3), 0], wz_s)
    drain(wfull.at[pl.ds(0, 3), :, 0], wx_s)
    drain(wfull.at[:, :, 0], wc_s)
    drain(rc, red_s.at[0])
    drain(rx.at[pl.ds(0, 3)], red_s.at[1])
    drain(rz.at[pl.ds(0, 3)], red_s.at[2])
    drain(rl, red_s.at[3])
    drain(ry.at[pl.ds(0, NY - 1)], red_s.at[4])
    drain(ry.at[pl.ds(0, NY - 1)], red_s.at[5])


def copy_out(*refs):
    n = (len(refs) - 2) // 3
    sources, targets, held = refs[:n], refs[n : 2 * n], refs[2 * n : 3 * n]
    in_sem, out_sem = refs[3 * n :]
    inward = [pltpu.make_async_copy(sources[i], held[i], in_sem.at[i]) for i in range(n)]
    outward = [pltpu.make_async_copy(held[i], targets[i], out_sem.at[i]) for i in range(n)]
    for copy in inward:
        copy.start()
    for i in range(n):
        inward[i].wait()
        outward[i].start()
    for copy in outward:
        copy.wait()


def shards(q, k, v, blocks, w, a, b, cot):
    hbm = pl.BlockSpec(memory_space=pl.ANY)
    vmem = pl.BlockSpec(memory_space=pltpu.VMEM)
    smem = pl.BlockSpec(memory_space=pltpu.SMEM)
    dma = pltpu.SemaphoreType.DMA
    blocks3 = pltpu.VMEM((NB, BLOCK, BLOCK), BF16)
    tokens = jax.ShapeDtypeStruct((BLOCK, MODEL_WIDTH), BF16)
    grad = jax.ShapeDtypeStruct((SHARD, ADAPTER_RANK), F32)
    outs = pl.pallas_call(
        kernel,
        out_shape=(tokens, tokens, tokens, tokens, grad, grad),
        in_specs=[hbm, hbm, hbm, smem, hbm, vmem, vmem, vmem],
        out_specs=(vmem, hbm, hbm, hbm, vmem, vmem),
        scratch_shapes=[
            blocks3,
            blocks3,
            blocks3,
            blocks3,
            blocks3,
            blocks3,
            pltpu.VMEM((BLOCK, MODEL_WIDTH), BF16),
            blocks3,
            blocks3,
            blocks3,
            pltpu.VMEM((NZ, NX, 2, SHARD, MODEL_WIDTH), BF16),
            pltpu.VMEM((NZ, NX, 2, SHARD, 2 * ADAPTER_RANK), BF16),
            pltpu.VMEM((NB, KEY_BLOCKS * BLOCK, BLOCK), F32),
            pltpu.VMEM((NB, KEY_BLOCKS, BLOCK, BLOCK), BF16),
            pltpu.VMEM((NB, KEY_BLOCKS, BLOCK, BLOCK), BF16),
            pltpu.VMEM((RANDOM + 1, BLOCK, BLOCK), F32),
            pltpu.VMEM((RANDOM + 1, BLOCK, BLOCK), F32),
            pltpu.VMEM((BLOCK, 2 * ADAPTER_RANK), BF16),
            pltpu.VMEM((BLOCK, 2 * ADAPTER_RANK), BF16),
            pltpu.VMEM((NZ, NX, 2, SHARD, BLOCK), F32),
            pltpu.VMEM((NZ, NX, SHARD, BLOCK), F32),
            pltpu.VMEM((NZ, NX, SHARD, BLOCK), F32),
            pltpu.VMEM((NX, NZ, SHARD, BLOCK), F32),
            pltpu.VMEM((NZ, SHARD, BLOCK), F32),
            pltpu.VMEM((NZ, SHARD, BLOCK), F32),
            pltpu.VMEM((SHARD, BLOCK), F32),
            pltpu.VMEM((SHARD, BLOCK), F32),
            pltpu.VMEM((NY, 8, BLOCK), F32),
            pltpu.VMEM((NY, 8, BLOCK), F32),
            pltpu.VMEM((8, BLOCK), F32),
            pltpu.VMEM((NY, 8, BLOCK), F32),
            pltpu.SMEM((RANDOM,), jnp.int32),
            pltpu.SMEM((RANDOM,), jnp.int32),
            pltpu.SMEM((RANDOM,), F32),
            pltpu.SMEM((NB,), jnp.int32),
            pltpu.SMEM((NB,), F32),
            dma((3,)),
            dma((3,)),
            dma((5,)),
            dma((5,)),
            dma((3,)),
            dma((3,)),
            dma,
            dma((NZ,)),
            dma,
            dma((NZ, NX)),
            dma,
            dma((NZ, NX)),
            dma,
            dma((NB,)),
            dma((6,)),
            dma((6,)),
        ],
        compiler_params=pltpu.CompilerParams(
            collective_id=0, has_side_effects=True, vmem_limit_bytes=60 * 2**20
        ),
    )(q, k, v, jnp.transpose(blocks, (2, 0, 1)), w, a, b, cot)
    return pl.pallas_call(
        copy_out,
        out_shape=tuple(jax.ShapeDtypeStruct(o.shape, o.dtype) for o in outs),
        in_specs=[hbm] * len(outs),
        out_specs=(hbm,) * len(outs),
        scratch_shapes=[pltpu.VMEM(o.shape, o.dtype) for o in outs] + [dma((len(outs),)), dma((len(outs),))],
        compiler_params=pltpu.CompilerParams(vmem_limit_bytes=60 * 2**20),
    )(*outs)


def solution(mesh):
    rows = P(("fsdp", "sp"), None)
    return jax.shard_map(
        shards,
        mesh=mesh,
        in_specs=(rows, rows, rows, P("fsdp", None, None), P("fsdp", None), P("fsdp", None), P("fsdp", None), rows),
        out_specs=(rows, rows, rows, rows, P("fsdp", None), P("fsdp", None)),
        check_vma=False,
    )
```
